128 devices in a mesh: labels: 32 (over z, y, core), queries: 4 (over x).
Axes of the slice: x: 4, y: 4, z: 4, core: 2. Of those that a mesh axis runs over, the one named last changes fastest.
Arguments:
- queries_in: bfloat16 [32768, 768], P(('queries', 'labels')), may hold values from -6 to 6
- classifier: bfloat16 [65536, 768], P('labels'), may hold values from -0.21875 to 0.21875
- owner_ids: int32 [32768, 8], P(('queries', 'labels')), may hold values from 0 to 31, all different within a row; in each aligned block of 256 rows (0 to 255, 256 to 511, ...) at most 128 rows name the same one
- local_ids: int32 [32768, 8], P(('queries', 'labels')), may hold values from 0 to 15
- targets: int32 [32768, 8, 128], P(('queries', 'labels')), may hold values 0 or 1
Outputs:
- query_loss: float32 [32768], P(('queries', 'labels'))
- feature_grad: float32 [32768, 768], P(('queries', 'labels'))
- weight_grad: bfloat16 [65536, 768], P(('labels', 'queries'))
The draws below stay inside these ranges and needn't reach their ends.
Inputs may be any that keep to these rules, and one draw needn't show every extreme that they name: `owner_ids`: each row names 8 different owners. Among the rows of one device no owner is named by more than 128 rows, a bound that some block reaches.
All inputs are finite; a program needn't handle non-finite values. No bound on the sum of `targets` on one device may be relied on, other than what follows from the above.
Results may differ from the reference program's by a relative error of at most 0.0065.
Values may be sent and summed in bfloat16 or wider, within the bound.
A program may use at most 320 MiB of HBM per device.

```python
import math
import jax
import jax.numpy as jnp
import numpy as np
from jax import lax

D = 768
BLOCK = 128
TOP = 8
BLK_DEV = 16
Q_DEV = 256
CAP = 128
BLOCKS = 512
LABELS = 65536
QUERIES = 32768
N_LABELS = 32


def place_ends(drawn, own_key, least, high):
    dims = drawn.shape
    spot = [jax.random.randint(jax.random.fold_in(own_key, axis), (), 0, dims[axis]) for axis in range(len(dims))]
    drawn = drawn.at[tuple(spot)].set(least)
    longest = dims.index(max(dims))
    spot[longest] = (spot[longest] + 1) % dims[longest]
    return drawn.at[tuple(spot)].set(high)


def shard_levels(key, shape, split, low, high):
    gain, own = 1.0, jax.random.fold_in(key, 6)
    for dim, blocks in split:
        draws = jnp.exp(jax.random.uniform(jax.random.fold_in(own, dim), (blocks,), jnp.float32, low / len(split), high / len(split)))
        gain = gain * jnp.repeat(draws, shape[dim] // blocks).reshape([-1 if axis == dim else 1 for axis in range(len(shape))])
    return gain


def cumulative_ranks(amount, skew):
    portions = [(1 << 20) // math.isqrt(standing ** skew) + 1 for standing in range(1, amount + 1)]
    deviation = 1 + sum(portions) // (1 << 30)
    return np.cumsum(np.array([max(1, weight // deviation) for weight in portions]))


def ranked(rng, dims, number_of, skew):
    table = cumulative_ranks(number_of, skew)
    lot = jax.random.randint(jax.random.fold_in(rng, 1), dims, 0, int(table[number_of - 1]))
    grade = jnp.searchsorted(jnp.asarray(table, jnp.int32), lot, side="right")
    return jax.random.permutation(jax.random.fold_in(rng, 2), number_of)[grade].astype(jnp.int32)


def routed_block(own_key, own, number, rows, count, top, most, lean):
    ranking = jax.random.permutation(own_key, count)
    packed, common = load_shares(count, rows * top, most, lean, True), load_shares(count, rows * top, most, lean, False)
    places = jnp.arange(count)

    def named(tallies, rotation):
        used = int((tallies > 0).sum())
        fixed = max(1, used // 4)
        passed = fixed + (places - fixed + rotation * (used - fixed)) % max(1, count - fixed)
        return jnp.zeros((count,), jnp.int32).at[ranking[jnp.where(places < fixed, places, passed)]].set(jnp.asarray(tallies, jnp.int32))

    tallies = jnp.where(number % 4 == 0, named(packed, number // 4), named(common, number - number // 4 - 1))
    mixed = jax.random.permutation(jax.random.fold_in(own, 3), count)
    donor, receiver = mixed[0:count // 2 * 2:2], mixed[1:count // 2 * 2:2]
    margin = jnp.minimum(tallies[donor] - 1, most - tallies[receiver]) // 2
    margin = jnp.where((donor == ranking[0]) | (receiver == ranking[0]) | (tallies[receiver] == 0), 0, jnp.maximum(margin, 0))
    passed = jax.random.randint(jax.random.fold_in(own, 4), (count // 2,), 0, 1 << 20) % (margin + 1)
    tallies = tallies.at[donor].add(-passed).at[receiver].add(passed)
    members = jnp.searchsorted(jnp.cumsum(tallies), jnp.arange(rows * top), side="right").astype(jnp.int32)
    listing = members.reshape(top, rows).T
    listing = listing[jax.random.permutation(jax.random.fold_in(own, 1), rows)]
    rotation = jax.random.randint(jax.random.fold_in(own, 2), (rows, 1), 0, top)
    return jnp.take_along_axis(listing, (jnp.arange(top)[None, :] + rotation) % top, axis=1)


def load_shares(number_of, total, limit, lean, full):
    weights = [(1 << 20) // math.isqrt(rank ** lean) + 1 for rank in range(1, number_of + 1)]
    largest = limit if full else min(limit, max(-(-total // number_of), total * weights[0] // sum(weights)))
    least = 1 if total - largest >= number_of - 1 else 0
    counts, rest = [largest] + [least] * (number_of - 1), total - largest - least * (number_of - 1)
    while rest > 0:
        free = [i for i in range(1, number_of) if counts[i] < largest] or [i for i in range(1, number_of) if counts[i] < limit]
        whole, left = sum([weights[i] for i in free]), rest
        for i in free:
            more = min(limit - counts[i], max(1, left * weights[i] // whole), rest)
            counts[i] = counts[i] + more
            rest = rest - more
    return np.array(counts)


def centred(key, dims, deviation, limit, shards=(), kind=jnp.bfloat16):
    drawn = deviation * jax.random.normal(key, dims, jnp.float32)
    if shards:
        drawn = drawn * shard_levels(key, dims, shards, -0.22, 0.18)
    return jnp.clip(drawn, -limit, limit).astype(kind)


def setup_inputs(seed: int = 0) -> dict:
    splits = jax.random.split(jax.random.key(seed), 6)
    queries_in = centred(splits[0], (QUERIES, D), 1.0, 6.0, ((0, 128),))
    classifier = centred(splits[1], (LABELS, D), D ** -0.5, 0.21875, ((0, 32),))
    owner_ids_keys = jax.random.split(jax.random.fold_in(splits[2], 1), QUERIES // Q_DEV)
    owner_ids_turns = jax.random.permutation(jax.random.fold_in(splits[2], 3), QUERIES // Q_DEV)
    owner_ids = jax.vmap(lambda own, number: routed_block(jax.random.fold_in(splits[2], 2), own, number, Q_DEV, N_LABELS, TOP, CAP, 2))(owner_ids_keys, owner_ids_turns).reshape((QUERIES, TOP))
    local_ids = place_ends(ranked(splits[3], (QUERIES, TOP), BLK_DEV, 2), jax.random.fold_in(splits[3], 3), 0, BLK_DEV - 1).astype(jnp.int32)
    targets = place_ends((jax.random.randint(splits[4], (QUERIES, TOP, BLOCK), 0, 3) < 1).astype(jnp.int32), jax.random.fold_in(splits[4], 1), 0, 1)
    return {"queries_in": queries_in, "classifier": classifier, "owner_ids": owner_ids, "local_ids": local_ids, "targets": targets}


loss_scale = 0.25


def reference(queries_in, classifier, owner_ids, local_ids, targets):
    block_id = (owner_ids * BLK_DEV + local_ids).astype(jnp.int32)
    weight_blocks = classifier.reshape(BLOCKS, BLOCK, D)
    tile_count = QUERIES // Q_DEV
    feature_tiles = queries_in.reshape(tile_count, Q_DEV, D)
    block_tiles = block_id.reshape(tile_count, Q_DEV, TOP)
    target_label_tiles = targets.reshape(tile_count, Q_DEV, TOP, BLOCK)

    def advance(running, inputs):
        feature_matrix, blocks_now, target_now = inputs
        gathered = weight_blocks[blocks_now].astype(jnp.float32)
        feature_float = feature_matrix.astype(jnp.float32)
        scores = jnp.einsum("cd,ctkd->ctk", feature_float, gathered).astype(jnp.bfloat16)
        scores = lax.optimization_barrier(scores).astype(jnp.float32)
        label_float = target_now.astype(jnp.float32)
        loss_now = jnp.sum(jax.nn.softplus(scores) - label_float * scores, axis=(1, 2)) * loss_scale
        loss_grads = ((jax.nn.sigmoid(scores) - label_float) * loss_scale).astype(jnp.bfloat16)
        grad_float = lax.optimization_barrier(loss_grads).astype(jnp.float32)
        block_terms = jnp.einsum("ctk,ctkd->ctd", grad_float, gathered).astype(jnp.bfloat16)
        feature_now = jnp.sum(block_terms.astype(jnp.float32), axis=1)
        outer_terms = jnp.einsum("ctk,cd->ctkd", grad_float, feature_float)
        running = running.at[blocks_now.reshape(-1)].add(outer_terms.reshape(-1, BLOCK, D))
        return running, (loss_now, feature_now)

    start_grad = jnp.zeros((BLOCKS, BLOCK, D), jnp.float32)
    summed, (loss_tiles, feature_tiles_out) = lax.scan(advance, start_grad, (feature_tiles, block_tiles, target_label_tiles))
    query_loss = loss_tiles.reshape(QUERIES)
    feature_grad = feature_tiles_out.reshape(QUERIES, D)
    weight_grad = summed.reshape(LABELS, D).astype(jnp.bfloat16)
    return query_loss, feature_grad, weight_grad
```

```python
import jax
import jax.numpy as jnp
from jax import lax
from jax.experimental import pallas as pl
from jax.experimental.pallas import tpu as pltpu
from jax.sharding import PartitionSpec as P

MESH = pl.DeviceIdType.MESH
BF = jnp.bfloat16
F32 = jnp.float32

ORDER = [
    (0, 0), (0, 1), (1, 0), (0, 3), (3, 0), (0, 2), (2, 0), (1, 1),
    (1, 3), (3, 1), (1, 2), (2, 1), (3, 3), (3, 2), (2, 3), (2, 2),
]
SLOT = {chip: k for k, chip in enumerate(ORDER)}
MIRROR = [SLOT[(b, a)] for a, b in ORDER]
PAY = 144


def slot(a, b):
    return SLOT[(a % 4, b % 4)]


def nt(a, b):
    return lax.dot_general(a, b, (((1,), (1,)), ((), ())), preferred_element_type=F32)


def nn(a, b):
    return jnp.dot(a, b, preferred_element_type=F32)


def one_chunk(k, own, sib, pay, w, wt, rows, grads, terms0, terms1, loss_out):
    half = lax.rem(k, 2)
    spot = lax.broadcasted_iota(jnp.int32, (128, 128), 0).astype(F32) + 1.0
    picks, ids = [], []
    for core, src in enumerate((own, sib)):
        tail = pay[core, k, 128:144, :].astype(F32)
        ids.append(tail[0:1, :])
        pick = jnp.concatenate(
            [jnp.where(spot == tail[r : r + 1, :], 1.0, 0.0) for r in (1, 2)], axis=1
        )
        picks.append(pick)
        rows[half, core * 128 : core * 128 + 128, :] = nn(pick.astype(BF), src[k]).astype(BF)
    ids = jnp.concatenate(ids, axis=1)
    x = rows[half]
    z = jnp.zeros((128, 256), F32)
    for part in range(2):
        scores = nt(w[part * 1024 : part * 1024 + 1024, :], x)
        for b in range(8):
            z = jnp.where(ids == float(part * 8 + b + 1), scores[b * 128 : b * 128 + 128, :], z)
    z = z.astype(BF).astype(F32)
    y = jnp.concatenate([pay[core, k, 0:128, :] for core in (0, 1)], axis=1).astype(F32)
    valid = jnp.where(ids > 0.5, 0.25, 0.0)
    e = jnp.exp(-jnp.abs(z))
    loss = jnp.sum(jnp.maximum(z, 0.0) + jnp.log1p(e) - y * z, axis=0, keepdims=True) * valid
    sig = jnp.where(z >= 0.0, 1.0, e) / (1.0 + e)
    g = (sig - y) * valid
    for b in range(16):
        grads[half, b * 128 : b * 128 + 128, :] = jnp.where(ids == float(b + 1), g, 0.0).astype(BF)
    ft = nn(wt[...], grads[half]).astype(BF)
    place = lax.broadcasted_iota(jnp.int32, (16, 128), 0)
    for core, terms in enumerate((terms0, terms1)):
        index = k if core == 0 else lax.rem(k, 4)
        pick = picks[core]
        terms[index] = nt(pick.T.astype(BF), ft[:, core * 128 : core * 128 + 128]).astype(BF)
        part = loss[:, core * 128 : core * 128 + 128]
        high = part.astype(BF).astype(F32)
        mid = (part - high).astype(BF).astype(F32)
        low = part - high - mid
        stack = jnp.where(place == 0, high, jnp.where(place == 1, mid, jnp.where(place == 2, low, 0.0)))
        spread = nn(stack.astype(BF), pick.astype(BF))
        loss_out[core, k] = jnp.broadcast_to(jnp.sum(spread, axis=0, keepdims=True), (8, 256))


def add_weight(rows, grads, total):
    def step(m, _):
        at = pl.ds(pl.multiple_of(m * 512, 512), 512)
        total[at, :] += nn(grads[0, at, :], rows[0]) + nn(grads[1, at, :], rows[1])
        return 0

    lax.fori_loop(0, 4, step, 0)


def kernel(
    q_ref, w, wt, labels_in, owner_ref, rank_ref, tail_ref,
    loss_ref, feat_ref, weight_ref,
    own, sib, pay_out, pay, terms0, terms1, back, half_in, full_in, half_a, full_a,
    total, half_x, full_x, rows, grads, loss_out, loss_in,
    own_s, own_r, sib_s, sib_r, pay_s, pay_r, back_s, back_r, rs_s, rs_r, loss_s, loss_r,
):
    me = lax.axis_index("labels")
    mx = lax.axis_index("queries")
    core = lax.rem(me, 2)
    my = lax.rem(me // 2, 4)
    mz = me // 8

    def dev(a, b, c=0):
        dz = a * (1 - core) + b * core
        dy = b * (1 - core) + a * core
        return (lax.rem(mz + dz, 4) * 4 + lax.rem(my + dy, 4)) * 2 + lax.rem(core + c, 2)

    def to(device, src, dst, ssem, rsem):
        return pltpu.make_async_remote_copy(
            src_ref=src, dst_ref=dst, send_sem=ssem, recv_sem=rsem,
            device_id={"labels": device}, device_id_type=MESH,
        )

    def to_x(step, src, dst, ssem, rsem):
        return pltpu.make_async_remote_copy(
            src_ref=src, dst_ref=dst, send_sem=ssem, recv_sem=rsem,
            device_id={"queries": lax.rem(mx + step, 4)}, device_id_type=MESH,
        )

    barrier = pltpu.get_barrier_semaphore()

    def greet(i, _):
        pl.semaphore_signal(
            barrier, inc=1, device_id={"labels": lax.rem(me + i, 32)}, device_id_type=MESH
        )
        return 0

    lax.fori_loop(1, 32, greet, 0)
    for step in (1, 3):
        pl.semaphore_signal(
            barrier, inc=1, device_id={"queries": lax.rem(mx + step, 4)}, device_id_type=MESH
        )
    pl.semaphore_wait(barrier, 33)

    sent = []

    def go(make):
        make().start()
        sent.append(make)

    def rows_of(ref, half):
        return ref if half is None else ref.at[pl.ds(half * 128, 128), :]

    def pass_on(k):
        a, b = ORDER[k]
        sends = []
        if b == 0:
            if a == 0:
                sends += [(1, 0, None), (3, 0, None)]
            if a == 3:
                sends.append((1, 0, 0))
            if a == 1:
                sends.append((3, 0, 1))
            sends += [(0, 1, None), (0, 3, None)]
        if b == 3:
            sends.append((0, 1, 0))
        if b == 1:
            sends.append((0, 3, 1))
        for n, (sa, sb, half) in enumerate(sends):
            there = slot(a - sa, b - sb)
            go(
                lambda sa=sa, sb=sb, half=half, there=there, n=n: to(
                    dev(sa, sb),
                    rows_of(own.at[k], half),
                    rows_of(own.at[there], half),
                    own_s.at[k * 4 + n],
                    own_r.at[there * 2 + (half or 0)],
                )
            )
        go(lambda: to(dev(0, 0, 1), own.at[k], sib.at[MIRROR[k]], sib_s.at[k], sib_r.at[MIRROR[k]]))

    def arrive(k):
        a, b = ORDER[k]
        halves = (0, 1) if b == 2 or (b == 0 and a == 2) else (None,)
        for half in halves:
            ref = rows_of(own.at[k], half)
            to(dev(0, 0, 1), ref, ref, own_s.at[k * 4], own_r.at[k * 2 + (half or 0)]).wait_recv()
        pass_on(k)

    own[0] = q_ref[...]
    pass_on(0)

    spot = lax.broadcasted_iota(jnp.int32, (128, 2048), 0)
    first = lax.broadcasted_iota(jnp.int32, (16, 128), 0) == 0

    def pack(group, _):
        owners = owner_ref[...]
        ranks = rank_ref[...]
        stack = jnp.concatenate(
            [
                jnp.where(spot == jnp.where(owners == group * 4 + i, ranks, -1), 1.0, 0.0).astype(BF)
                for i in range(4)
            ],
            axis=0,
        )
        found = nn(stack, labels_in[...])
        for i in range(4):
            piece = found[i * 128 : i * 128 + 128, :]
            o = group * 4 + i
            pay_out[o, 0:128, :] = piece[:, 0:128].T.astype(BF)
            ids = piece[:, 128:256].T[0:16, :]
            pay_out[o, 128:144, :] = (jnp.where(first, ids, 0.0) + tail_ref[o]).astype(BF)
        return 0

    lax.fori_loop(0, 8, pack, 0)
    pay[0, 0] = pay_out[me]
    for k, (a, b) in enumerate(ORDER):
        for c in (0, 1):
            if k == 0 and c == 0:
                continue
            there = slot(-a, -b) if c == 0 else slot(-b, -a)

            def make(a=a, b=b, c=c, k=k, there=there):
                d = dev(a, b, c)
                return to(d, pay_out.at[d], pay.at[c, there], pay_s.at[c * 16 + k], pay_r.at[c * 16 + there])

            go(make)

    def halves_of(buf, index, a_axis, store, sem):
        for h in (0, 1):
            step = 1 if h == 0 else 3
            d = (step, 0) if a_axis else (0, step)
            go(
                lambda d=d, h=h: to(
                    dev(*d), rows_of(buf.at[index], h), store(h), rs_s.at[sem + h], rs_r.at[sem + h]
                )
            )

    def fulls_of(buf, plus, minus, a_axis, store, sem):
        for h, index in enumerate((plus, minus)):
            step = 1 if h == 0 else 3
            d = (step, 0) if a_axis else (0, step)
            go(
                lambda d=d, h=h, index=index: to(
                    dev(*d), buf.at[index], store(h), rs_s.at[sem + 2 + h], rs_r.at[sem + 2 + h]
                )
            )

    def got(store, h, sem):
        to(dev(0, 0, 1), store(h), store(h), rs_s.at[sem], rs_r.at[sem]).wait_recv()

    def stage1(a):
        for b in (2, 1, 3, 0):
            k = slot(a, b)
            far = MIRROR[k]
            to(dev(0, 0, 1), back.at[far], back.at[far], back_s.at[far], back_r.at[far]).wait_recv()
            terms0[k] = terms0[k] + back[far]
            if b == 2:
                halves_of(terms0, k, False, lambda h: half_in.at[a, h], a * 4)

    def meet(buf, plus, minus, store, sem):
        got(store, 0, sem)
        buf[plus, 0:128, :] = buf[plus, 0:128, :] + store(0)[...]
        got(store, 1, sem + 1)
        buf[minus, 128:256, :] = buf[minus, 128:256, :] + store(1)[...]

    def stage2(a):
        plus, minus = slot(a, 1), slot(a, 3)
        meet(terms0, plus, minus, lambda h: half_in.at[a, h], a * 4)
        fulls_of(terms0, plus, minus, False, lambda h: full_in.at[a, h], a * 4)

    def stage3(a):
        for h in (0, 1):
            got(lambda h: full_in.at[a, h], h, a * 4 + 2 + h)
        k = slot(a, 0)
        terms0[k] = (
            terms0[k].astype(F32) + full_in[a, 0].astype(F32) + full_in[a, 1].astype(F32)
        ).astype(BF)

    acts = {
        1: [lambda: [arrive(k) for k in (1, 2, 3, 4)]],
        3: [lambda: [arrive(k) for k in (5, 6)]],
        4: [lambda: [arrive(k) for k in (7, 8, 9, 12)]],
        6: [lambda: [arrive(k) for k in (10, 11, 13, 14)]],
        8: [lambda: stage1(0)],
        9: [lambda: arrive(15)],
        10: [lambda: stage2(0)],
        12: [lambda: stage3(0)],
        13: [lambda: stage1(1)],
        14: [lambda: stage2(1)],
        15: [lambda: stage3(1), lambda: stage1(3)],
    }

    def send_back(k, index):
        return to(dev(0, 0, 1), terms1.at[index], back.at[k], back_s.at[k], back_r.at[k])

    total[...] = jnp.zeros_like(total)

    def step(k, _):
        for when, todo in acts.items():

            @pl.when(k == when)
            def _():
                for act in todo:
                    act()

        to(dev(0, 0, 1), sib.at[k], sib.at[k], sib_s.at[k], sib_r.at[k]).wait_recv()

        @pl.when(k > 0)
        def _():
            to(dev(0, 0, 1), pay.at[0, k], pay.at[0, k], pay_s.at[k], pay_r.at[k]).wait_recv()

        to(dev(0, 0, 1), pay.at[1, k], pay.at[1, k], pay_s.at[16 + k], pay_r.at[16 + k]).wait_recv()

        @pl.when(k >= 4)
        def _():
            send_back(k - 4, lax.rem(k, 4)).wait_send()

        one_chunk(k, own, sib, pay, w, wt, rows, grads, terms0, terms1, loss_out)
        send_back(k, lax.rem(k, 4)).start()

        @pl.when(lax.rem(k, 2) == 1)
        def _():
            add_weight(rows, grads, total)

        return 0

    lax.fori_loop(0, 16, step, 0)
    for k in range(12, 16):
        send_back(k, k % 4).wait_send()

    def shard(dx):
        return pl.ds(pl.multiple_of(lax.rem(mx + dx, 4) * 512, 512), 512)

    for dx in (2, 1, 3):
        block = total[shard(dx), :].astype(BF)
        for h in (0, 1):
            sib[(dx - 1) * 2 + h] = block[h * 256 : h * 256 + 256, :]
        if dx == 2:
            for h in (0, 1):
                go(
                    lambda h=h: to_x(
                        1 if h == 0 else 3, sib.at[2 + h], half_x.at[h], rs_s.at[20 + h], rs_r.at[20 + h]
                    )
                )
    stage1(2)

    for k, (a, b) in enumerate(ORDER):
        for c in (0, 1):
            if k == 0 and c == 0:
                continue
            there = slot(-a, -b) if c == 0 else slot(-b, -a)
            go(
                lambda a=a, b=b, c=c, k=k, there=there: to(
                    dev(a, b, c), loss_out.at[c, k], loss_in.at[c, there],
                    loss_s.at[c * 16 + k], loss_r.at[c * 16 + there],
                )
            )
    stage2(3)
    for h in (0, 1):
        to_x(1, half_x.at[h], half_x.at[h], rs_s.at[20 + h], rs_r.at[20 + h]).wait_recv()
    sib[0] = sib[0] + half_x[0]
    sib[5] = sib[5] + half_x[1]
    for h in (0, 1):
        go(
            lambda h=h: to_x(
                1 if h == 0 else 3,
                sib.at[pl.ds(0 if h == 0 else 4, 2)], full_x.at[h], rs_s.at[22 + h], rs_r.at[22 + h],
            )
        )
    stage2(2)
    stage3(3)
    stage3(2)
    halves_of(terms0, slot(2, 0), True, lambda h: half_a.at[h], 16)
    plus, minus = slot(1, 0), slot(3, 0)
    meet(terms0, plus, minus, lambda h: half_a.at[h], 16)
    fulls_of(terms0, plus, minus, True, lambda h: full_a.at[h], 16)

    loss = loss_out[0, 0]
    for k in range(16):
        for c in (0, 1):
            if k == 0 and c == 0:
                continue
            ref = loss_in.at[c, k]
            to(dev(0, 0, 1), ref, ref, loss_s.at[c * 16 + k], loss_r.at[c * 16 + k]).wait_recv()
            loss = loss + loss_in[c, k]
    loss_ref[...] = loss

    for h in (0, 1):
        got(lambda h: full_a.at[h], h, 18 + h)
    feat_ref[...] = terms0[0].astype(F32) + full_a[0].astype(F32) + full_a[1].astype(F32)

    for h in (0, 1):
        to_x(1, full_x.at[h], full_x.at[h], rs_s.at[22 + h], rs_r.at[22 + h]).wait_recv()
    for h in (0, 1):
        at = pl.ds(pl.multiple_of(mx * 512 + h * 256, 256), 256)
        weight_ref[h * 256 : h * 256 + 256, :] = (
            total[at, :] + full_x[0, h].astype(F32) + full_x[1, h].astype(F32)
        ).astype(BF)

    for make in sent:
        make().wait_send()


def shards(queries_in, classifier, owner_ids, local_ids, targets):
    rows, width = queries_in.shape
    top = owner_ids.shape[1]
    pairs = rows * top
    hot = owner_ids[:, :, None] == jnp.arange(32, dtype=jnp.int32)[None, None, :]
    hit = jnp.any(hot, axis=1)
    before = jnp.tril(jnp.ones((rows, rows), BF), -1)
    rank = jnp.dot(before, hit.astype(BF), preferred_element_type=F32)
    ranks = jnp.sum(jnp.where(hot, rank[:, None, :], 0.0), axis=2).astype(jnp.int32)
    slots = jnp.where(hit, rank + 1.0, 0.0).T.reshape(32, 2, 128)
    tail = jnp.pad(slots, ((0, 0), (1, 13), (0, 0)))
    ids = jnp.broadcast_to((local_ids + 1).reshape(pairs, 1), (pairs, 128))
    labels_in = jnp.concatenate([targets.reshape(pairs, 128), ids], axis=1).astype(BF)
    vmem = pl.BlockSpec(memory_space=pltpu.VMEM)
    block = (rows, width)
    loss, feat, weight = pl.pallas_call(
        kernel,
        out_shape=(
            jax.ShapeDtypeStruct((8, rows), F32),
            jax.ShapeDtypeStruct(block, F32),
            jax.ShapeDtypeStruct((512, width), BF),
        ),
        in_specs=[vmem] * 7,
        out_specs=(vmem, vmem, vmem),
        scratch_shapes=[
            pltpu.VMEM((16, *block), BF),
            pltpu.VMEM((16, *block), BF),
            pltpu.VMEM((32, PAY, 128), BF),
            pltpu.VMEM((2, 16, PAY, 128), BF),
            pltpu.VMEM((16, *block), BF),
            pltpu.VMEM((4, *block), BF),
            pltpu.VMEM((16, *block), BF),
            pltpu.VMEM((4, 2, 128, width), BF),
            pltpu.VMEM((4, 2, *block), BF),
            pltpu.VMEM((2, 128, width), BF),
            pltpu.VMEM((2, *block), BF),
            pltpu.VMEM((2048, width), F32),
            pltpu.VMEM((2, 256, width), BF),
            pltpu.VMEM((2, 2, 256, width), BF),
            pltpu.VMEM((2, 256, width), BF),
            pltpu.VMEM((2, 2048, 256), BF),
            pltpu.VMEM((2, 16, 8, rows), F32),
            pltpu.VMEM((2, 16, 8, rows), F32),
            pltpu.SemaphoreType.DMA((64,)),
            pltpu.SemaphoreType.DMA((32,)),
            pltpu.SemaphoreType.DMA((16,)),
            pltpu.SemaphoreType.DMA((16,)),
            pltpu.SemaphoreType.DMA((32,)),
            pltpu.SemaphoreType.DMA((32,)),
            pltpu.SemaphoreType.DMA((16,)),
            pltpu.SemaphoreType.DMA((16,)),
            pltpu.SemaphoreType.DMA((24,)),
            pltpu.SemaphoreType.DMA((24,)),
            pltpu.SemaphoreType.DMA((32,)),
            pltpu.SemaphoreType.DMA((32,)),
        ],
        compiler_params=pltpu.CompilerParams(
            collective_id=0, has_side_effects=True, vmem_limit_bytes=64 * 1024 * 1024 - 65536
        ),
    )(
        queries_in, classifier, classifier.T, labels_in,
        owner_ids.reshape(1, pairs), ranks.reshape(1, pairs), tail,
    )
    return loss[0], feat, weight


def solution(mesh):
    in_specs = (
        P(("queries", "labels"), None),
        P("labels", None),
        P(("queries", "labels"), None),
        P(("queries", "labels"), None),
        P(("queries", "labels"), None, None),
    )
    out_specs = (
        P(("queries", "labels")),
        P(("queries", "labels"), None),
        P(("labels", "queries"), None),
    )
    return jax.shard_map(shards, mesh=mesh, in_specs=in_specs, out_specs=out_specs, check_vma=False)
```

```python
import jax
import jax.numpy as jnp
from jax import lax
from jax.experimental import pallas as pl
from jax.experimental.pallas import tpu as pltpu
from jax.sharding import PartitionSpec as P

MESH = pl.DeviceIdType.MESH
BF = jnp.bfloat16
F32 = jnp.float32

ORDER = [
    (0, 0), (0, 1), (1, 0), (0, 3), (3, 0), (0, 2), (2, 0), (1, 1),
    (1, 3), (3, 1), (1, 2), (2, 1), (3, 3), (3, 2), (2, 3), (2, 2),
]
SLOT = {chip: k for k, chip in enumerate(ORDER)}
MIRROR = [SLOT[(b, a)] for a, b in ORDER]
PAY = 144


def slot(a, b):
    return SLOT[(a % 4, b % 4)]


def nt(a, b):
    return lax.dot_general(a, b, (((1,), (1,)), ((), ())), preferred_element_type=F32)


def nn(a, b):
    return jnp.dot(a, b, preferred_element_type=F32)


def tn(a, b):
    return lax.dot_general(a, b, (((0,), (0,)), ((), ())), preferred_element_type=F32)


def pick_of(pay, core, k):
    spot = lax.broadcasted_iota(jnp.int32, (128, 128), 0).astype(F32) + 1.0
    tail = pay[core, k, 128:144, :].astype(F32)
    return jnp.concatenate(
        [jnp.where(spot == tail[r : r + 1, :], 1.0, 0.0) for r in (1, 2)], axis=1
    ).astype(BF)


def make_grads(k, own, sib, pay, w, rows, grads, loss_out):
    picks = [pick_of(pay, core, k) for core in (0, 1)]
    for core, src in enumerate((own, sib)):
        rows[core * 128 : core * 128 + 128, :] = nn(picks[core], src[k]).astype(BF)
    ids = jnp.concatenate(
        [pay[core, k, 128:144, :].astype(F32)[0:1, :] for core in (0, 1)], axis=1
    )
    x = rows[...]
    z = jnp.zeros((128, 256), F32)
    for part in range(2):
        scores = nt(w[part * 1024 : part * 1024 + 1024, :], x)
        for b in range(8):
            z = jnp.where(ids == float(part * 8 + b + 1), scores[b * 128 : b * 128 + 128, :], z)
    z = z.astype(BF).astype(F32)
    y = jnp.concatenate([pay[core, k, 0:128, :] for core in (0, 1)], axis=1).astype(F32)
    valid = jnp.where(ids > 0.5, 0.25, 0.0)
    e = jnp.exp(-jnp.abs(z))
    loss = jnp.sum(jnp.maximum(z, 0.0) + jnp.log1p(e) - y * z, axis=0, keepdims=True) * valid
    sig = jnp.where(z >= 0.0, 1.0, e) / (1.0 + e)
    g = ((sig - y) * valid).astype(BF).reshape(8, 16, 256)
    many = jnp.broadcast_to(ids, (16, 256))
    for b in range(16):
        hot = jnp.where(many == float(b + 1), 1.0, 0.0).astype(BF)
        grads[b * 128 : b * 128 + 128, :] = (g * hot[None]).reshape(128, 256)
    place = lax.broadcasted_iota(jnp.int32, (16, 128), 0)
    for core in (0, 1):
        part = loss[:, core * 128 : core * 128 + 128]
        high = part.astype(BF).astype(F32)
        mid = (part - high).astype(BF).astype(F32)
        low = part - high - mid
        stack = jnp.where(place == 0, high, jnp.where(place == 1, mid, jnp.where(place == 2, low, 0.0)))
        spread = nn(stack.astype(BF), picks[core])
        loss_out[core, k] = jnp.broadcast_to(jnp.sum(spread, axis=0, keepdims=True), (8, 256))


def make_terms(k, pay, w, grads, terms0, terms1, index):
    f = tn(grads[...], w[...]).astype(BF)
    terms0[k] = tn(pick_of(pay, 0, k), f[0:128, :]).astype(BF)
    terms1[index] = tn(pick_of(pay, 1, k), f[128:256, :]).astype(BF)


def add_weight(part, rows, grads, total):
    at = slice(part * 1024, part * 1024 + 1024)
    left = jnp.concatenate([grads[0][at, :], grads[1][at, :]], axis=1)
    right = jnp.concatenate([rows[0][...], rows[1][...]], axis=0)
    total[at, :] += nn(left, right)


def kernel(
    q_ref, w, targets, owner_ref, local_ref,
    loss_ref, feat_ref, weight_ref,
    own, sib, pay_out, pay, terms0, terms1, back, half_in, full_in, half_a, full_a,
    total, half_x, full_x, rows0, rows1, rows2, rows3, grads0, grads1, grads2, grads3,
    loss_out, loss_in, labels_in, slots,
    own_s, own_r, sib_s, sib_r, pay_s, pay_r, back_s, back_r, rs_s, rs_r, loss_s, loss_r, known,
):
    me = lax.axis_index("labels")
    mx = lax.axis_index("queries")
    core = lax.rem(me, 2)
    my = lax.rem(me // 2, 4)
    mz = me // 8

    def dev(a, b, c=0):
        dz = a * (1 - core) + b * core
        dy = b * (1 - core) + a * core
        return (lax.rem(mz + dz, 4) * 4 + lax.rem(my + dy, 4)) * 2 + lax.rem(core + c, 2)

    def to(device, src, dst, ssem, rsem):
        return pltpu.make_async_remote_copy(
            src_ref=src, dst_ref=dst, send_sem=ssem, recv_sem=rsem,
            device_id={"labels": device}, device_id_type=MESH,
        )

    def to_x(step, src, dst, ssem, rsem):
        return pltpu.make_async_remote_copy(
            src_ref=src, dst_ref=dst, send_sem=ssem, recv_sem=rsem,
            device_id={"queries": lax.rem(mx + step, 4)}, device_id_type=MESH,
        )

    barrier = pltpu.get_barrier_semaphore()
    ring_a, ring_b = (dev(1, 0), dev(3, 0)), (dev(0, 1), dev(0, 3))
    for device in (*ring_a, *ring_b, dev(0, 0, 1)):
        pl.semaphore_signal(barrier, inc=1, device_id={"labels": device}, device_id_type=MESH)
    for step in (1, 3):
        pl.semaphore_signal(
            barrier, inc=1, device_id={"queries": lax.rem(mx + step, 4)}, device_id_type=MESH
        )
    pl.semaphore_wait(barrier, 7)

    def tell(index, devices):
        for device in devices:
            pl.semaphore_signal(
                known.at[index], inc=1, device_id={"labels": device}, device_id_type=MESH
            )

    def hear(index, count):
        pl.semaphore_wait(known.at[index], count)

    sent = []

    def go(make):
        make().start()
        sent.append(make)

    def rows_of(ref, half):
        return ref if half is None else ref.at[pl.ds(half * 128, 128), :]

    def pass_on(k):
        a, b = ORDER[k]
        sends = []
        if b == 0:
            if a == 0:
                sends += [(1, 0, None), (3, 0, None)]
            if a == 3:
                sends.append((1, 0, 0))
            if a == 1:
                sends.append((3, 0, 1))
            sends += [(0, 1, None), (0, 3, None)]
        if b == 3:
            sends.append((0, 1, 0))
        if b == 1:
            sends.append((0, 3, 1))
        for n, (sa, sb, half) in enumerate(sends):
            there = slot(a - sa, b - sb)
            go(
                lambda sa=sa, sb=sb, half=half, there=there, n=n: to(
                    dev(sa, sb),
                    rows_of(own.at[k], half),
                    rows_of(own.at[there], half),
                    own_s.at[k * 4 + n],
                    own_r.at[there * 2 + (half or 0)],
                )
            )
        go(lambda: to(dev(0, 0, 1), own.at[k], sib.at[MIRROR[k]], sib_s.at[k], sib_r.at[MIRROR[k]]))

    def arrive(k):
        a, b = ORDER[k]
        halves = (0, 1) if b == 2 or (b == 0 and a == 2) else (None,)
        for half in halves:
            ref = rows_of(own.at[k], half)
            to(dev(0, 0, 1), ref, ref, own_s.at[k * 4], own_r.at[k * 2 + (half or 0)]).wait_recv()
        pass_on(k)

    own[0] = q_ref[...]
    pass_on(0)

    tell(0, ring_a)
    lane = lax.broadcasted_iota(jnp.int32, (256, 128), 1)
    hit = jnp.zeros((256, 128), F32)
    owners = jnp.zeros((256, 128), F32)
    for t in range(8):
        named = jnp.broadcast_to(owner_ref[:, t : t + 1], (256, 128))
        hit = jnp.where(lane == named, 1.0, hit)
        owners = jnp.where(lane == t, named.astype(F32), owners)
        at = slice(t * 256, t * 256 + 256)
        labels_in[at, 0:128] = targets[pl.ds(t, 256, stride=8), :].astype(BF)
        labels_in[at, 128:256] = (
            jnp.broadcast_to(local_ref[:, t : t + 1], (256, 128)) + 1
        ).astype(F32).astype(BF)
    before = jnp.where(
        lax.broadcasted_iota(jnp.int32, (256, 256), 1) < lax.broadcasted_iota(jnp.int32, (256, 256), 0),
        1.0, 0.0,
    )
    rank = nn(before.astype(BF), hit.astype(BF))
    slots[...] = jnp.where(hit > 0.5, rank + 1.0, 0.0).T
    owners = owners.T[0:8, :]
    hear(0, 2)
    tell(1, ring_b)
    spot = lax.broadcasted_iota(jnp.int32, (128, 256), 0).astype(F32) + 1.0
    place = lax.broadcasted_iota(jnp.int32, (16, 128), 0)

    def pack(group, _):
        stacks = []
        for i in range(4):
            o = group * 4 + i
            mine = slots[pl.ds(o, 1), :]
            stacks.append(
                jnp.concatenate(
                    [
                        jnp.where(
                            spot == jnp.where(owners[t : t + 1, :] == o.astype(F32), mine, 0.0), 1.0, 0.0
                        ).astype(BF)
                        for t in range(8)
                    ],
                    axis=1,
                )
            )
        found = nn(jnp.concatenate(stacks, axis=0), labels_in[...])
        for i in range(4):
            o = group * 4 + i
            piece = found[i * 128 : i * 128 + 128, :]
            pay_out[o, 0:128, :] = piece[:, 0:128].T.astype(BF)
            ids = piece[:, 128:256].T[0:16, :]
            mine = slots[pl.ds(o, 1), :]
            tail = jnp.where(
                place == 0, ids,
                jnp.where(place == 1, mine[:, 0:128], jnp.where(place == 2, mine[:, 128:256], 0.0)),
            )
            pay_out[o, 128:144, :] = tail.astype(BF)
        return 0

    lax.fori_loop(0, 4, pack, 0)
    hear(1, 2)
    tell(2, ring_b)
    lax.fori_loop(4, 8, pack, 0)
    hear(2, 2)
    tell(3, (dev(0, 0, 1),))
    hear(3, 1)
    pay[0, 0] = pay_out[me]
    for k, (a, b) in enumerate(ORDER):
        for c in (0, 1):
            if k == 0 and c == 0:
                continue
            there = slot(-a, -b) if c == 0 else slot(-b, -a)

            def make(a=a, b=b, c=c, k=k, there=there):
                d = dev(a, b, c)
                return to(d, pay_out.at[d], pay.at[c, there], pay_s.at[c * 16 + k], pay_r.at[c * 16 + there])

            go(make)

    def halves_of(buf, index, a_axis, store, sem):
        for h in (0, 1):
            step = 1 if h == 0 else 3
            d = (step, 0) if a_axis else (0, step)
            go(
                lambda d=d, h=h: to(
                    dev(*d), rows_of(buf.at[index], h), store(h), rs_s.at[sem + h], rs_r.at[sem + h]
                )
            )

    def fulls_of(buf, plus, minus, a_axis, store, sem):
        for h, index in enumerate((plus, minus)):
            step = 1 if h == 0 else 3
            d = (step, 0) if a_axis else (0, step)
            go(
                lambda d=d, h=h, index=index: to(
                    dev(*d), buf.at[index], store(h), rs_s.at[sem + 2 + h], rs_r.at[sem + 2 + h]
                )
            )

    def got(store, h, sem):
        to(dev(0, 0, 1), store(h), store(h), rs_s.at[sem], rs_r.at[sem]).wait_recv()

    def stage1(a):
        for b in (2, 1, 3, 0):
            k = slot(a, b)
            far = MIRROR[k]
            to(dev(0, 0, 1), back.at[far], back.at[far], back_s.at[far], back_r.at[far]).wait_recv()
            terms0[k] = terms0[k] + back[far]
            if b == 2:
                halves_of(terms0, k, False, lambda h: half_in.at[a, h], a * 4)

    def meet(buf, plus, minus, store, sem):
        got(store, 0, sem)
        buf[plus, 0:128, :] = buf[plus, 0:128, :] + store(0)[...]
        got(store, 1, sem + 1)
        buf[minus, 128:256, :] = buf[minus, 128:256, :] + store(1)[...]

    def stage2(a):
        plus, minus = slot(a, 1), slot(a, 3)
        meet(terms0, plus, minus, lambda h: half_in.at[a, h], a * 4)
        fulls_of(terms0, plus, minus, False, lambda h: full_in.at[a, h], a * 4)

    def stage3(a):
        for h in (0, 1):
            got(lambda h: full_in.at[a, h], h, a * 4 + 2 + h)
        k = slot(a, 0)
        terms0[k] = (
            terms0[k].astype(F32) + full_in[a, 0].astype(F32) + full_in[a, 1].astype(F32)
        ).astype(BF)

    acts = {
        1: [lambda: [arrive(k) for k in (1, 2, 3, 4)]],
        3: [lambda: [arrive(k) for k in (5, 6)]],
        4: [lambda: [arrive(k) for k in (7, 8, 9, 12)]],
        6: [lambda: [arrive(k) for k in (10, 11, 13, 14)]],
        8: [lambda: arrive(15)],
        9: [lambda: stage1(0)],
        11: [lambda: stage2(0)],
        13: [lambda: stage3(0)],
        14: [lambda: stage1(1)],
        15: [lambda: stage2(1)],
    }

    def send_back(k, index):
        return to(dev(0, 0, 1), terms1.at[index], back.at[k], back_s.at[k], back_r.at[k])

    all_rows = (rows0, rows1, rows2, rows3)
    all_grads = (grads0, grads1, grads2, grads3)
    for ref in (*all_rows[2:], *all_grads[2:], total):
        ref[...] = jnp.zeros_like(ref)

    def step(j, _):
        for i in range(4):
            k = j * 4 + i
            for when, todo in acts.items():
                if when % 4 != i:
                    continue

                @pl.when(j == when // 4)
                def _():
                    for act in todo:
                        act()

            to(dev(0, 0, 1), sib.at[k], sib.at[k], sib_s.at[k], sib_r.at[k]).wait_recv()
            to(dev(0, 0, 1), pay.at[1, k], pay.at[1, k], pay_s.at[16 + k], pay_r.at[16 + k]).wait_recv()

            def mine():
                to(dev(0, 0, 1), pay.at[0, k], pay.at[0, k], pay_s.at[k], pay_r.at[k]).wait_recv()

            if i == 0:
                pl.when(j > 0)(mine)
            else:
                mine()

            last = (i - 1) % 4
            if i == 0:

                @pl.when(j > 1)
                def _():
                    send_back(k - 5, last).wait_send()

            else:

                @pl.when(j > 0)
                def _():
                    send_back(k - 5, last).wait_send()

            pair = 2 if i < 2 else 0
            make_grads(k, own, sib, pay, w, all_rows[i], all_grads[i], loss_out)
            make_terms(k - 1 + lax.div(16 - k, 16), pay, w, all_grads[last], terms0, terms1, last)
            add_weight(i % 2, all_rows[pair : pair + 2], all_grads[pair : pair + 2], total)
            if i == 0:

                @pl.when(j > 0)
                def _():
                    send_back(k - 1, last).start()

            else:
                send_back(k - 1, last).start()
        return 0

    lax.fori_loop(0, 4, step, 0)
    for part in (0, 1):
        add_weight(part, all_rows[2:], all_grads[2:], total)

    def shard(dx):
        return pl.ds(pl.multiple_of(lax.rem(mx + dx, 4) * 512, 512), 512)

    for dx in (2, 1, 3):
        block = total[shard(dx), :].astype(BF)
        for h in (0, 1):
            sib[(dx - 1) * 2 + h] = block[h * 256 : h * 256 + 256, :]
        if dx == 2:
            for h in (0, 1):
                go(
                    lambda h=h: to_x(
                        1 if h == 0 else 3, sib.at[2 + h], half_x.at[h], rs_s.at[20 + h], rs_r.at[20 + h]
                    )
                )
    send_back(11, 3).wait_send()
    make_terms(15, pay, w, grads3, terms0, terms1, 3)
    send_back(15, 3).start()
    stage3(1)
    stage1(3)
    stage1(2)

    for k, (a, b) in enumerate(ORDER):
        for c in (0, 1):
            if k == 0 and c == 0:
                continue
            there = slot(-a, -b) if c == 0 else slot(-b, -a)
            go(
                lambda a=a, b=b, c=c, k=k, there=there: to(
                    dev(a, b, c), loss_out.at[c, k], loss_in.at[c, there],
                    loss_s.at[c * 16 + k], loss_r.at[c * 16 + there],
                )
            )
    stage2(3)
    for h in (0, 1):
        to_x(1, half_x.at[h], half_x.at[h], rs_s.at[20 + h], rs_r.at[20 + h]).wait_recv()
    sib[0] = sib[0] + half_x[0]
    sib[5] = sib[5] + half_x[1]
    for h in (0, 1):
        go(
            lambda h=h: to_x(
                1 if h == 0 else 3,
                sib.at[pl.ds(0 if h == 0 else 4, 2)], full_x.at[h], rs_s.at[22 + h], rs_r.at[22 + h],
            )
        )
    stage2(2)
    stage3(3)
    stage3(2)
    halves_of(terms0, slot(2, 0), True, lambda h: half_a.at[h], 16)
    plus, minus = slot(1, 0), slot(3, 0)
    meet(terms0, plus, minus, lambda h: half_a.at[h], 16)
    fulls_of(terms0, plus, minus, True, lambda h: full_a.at[h], 16)

    loss = loss_out[0, 0]
    for k in range(16):
        for c in (0, 1):
            if k == 0 and c == 0:
                continue
            ref = loss_in.at[c, k]
            to(dev(0, 0, 1), ref, ref, loss_s.at[c * 16 + k], loss_r.at[c * 16 + k]).wait_recv()
            loss = loss + loss_in[c, k]
    loss_ref[...] = loss

    for h in (0, 1):
        got(lambda h: full_a.at[h], h, 18 + h)
    feat_ref[...] = terms0[0].astype(F32) + full_a[0].astype(F32) + full_a[1].astype(F32)

    for h in (0, 1):
        to_x(1, full_x.at[h], full_x.at[h], rs_s.at[22 + h], rs_r.at[22 + h]).wait_recv()
    for h in (0, 1):
        at = pl.ds(pl.multiple_of(mx * 512 + h * 256, 256), 256)
        weight_ref[h * 256 : h * 256 + 256, :] = (
            total[at, :] + full_x[0, h].astype(F32) + full_x[1, h].astype(F32)
        ).astype(BF)

    for k in range(12, 16):
        send_back(k, k % 4).wait_send()
    for make in sent:
        make().wait_send()


def shards(queries_in, classifier, owner_ids, local_ids, targets):
    rows, width = queries_in.shape
    top = owner_ids.shape[1]
    pairs = rows * top
    vmem = pl.BlockSpec(memory_space=pltpu.VMEM)
    block = (rows, width)
    loss, feat, weight = pl.pallas_call(
        kernel,
        out_shape=(
            jax.ShapeDtypeStruct((8, rows), F32),
            jax.ShapeDtypeStruct(block, F32),
            jax.ShapeDtypeStruct((512, width), BF),
        ),
        in_specs=[vmem] * 5,
        out_specs=(vmem, vmem, vmem),
        scratch_shapes=[
            pltpu.VMEM((16, *block), BF),
            pltpu.VMEM((16, *block), BF),
            pltpu.VMEM((32, PAY, 128), BF),
            pltpu.VMEM((2, 16, PAY, 128), BF),
            pltpu.VMEM((16, *block), BF),
            pltpu.VMEM((4, *block), BF),
            pltpu.VMEM((16, *block), BF),
            pltpu.VMEM((4, 2, 128, width), BF),
            pltpu.VMEM((4, 2, *block), BF),
            pltpu.VMEM((2, 128, width), BF),
            pltpu.VMEM((2, *block), BF),
            pltpu.VMEM((2048, width), F32),
            pltpu.VMEM((2, 256, width), BF),
            pltpu.VMEM((2, 2, 256, width), BF),
            *[pltpu.VMEM((256, width), BF)] * 4,
            *[pltpu.VMEM((2048, 256), BF)] * 4,
            pltpu.VMEM((2, 16, 8, rows), F32),
            pltpu.VMEM((2, 16, 8, rows), F32),
            pltpu.VMEM((pairs, 256), BF),
            pltpu.VMEM((128, rows), F32),
            pltpu.SemaphoreType.DMA((64,)),
            pltpu.SemaphoreType.DMA((32,)),
            pltpu.SemaphoreType.DMA((16,)),
            pltpu.SemaphoreType.DMA((16,)),
            pltpu.SemaphoreType.DMA((32,)),
            pltpu.SemaphoreType.DMA((32,)),
            pltpu.SemaphoreType.DMA((16,)),
            pltpu.SemaphoreType.DMA((16,)),
            pltpu.SemaphoreType.DMA((24,)),
            pltpu.SemaphoreType.DMA((24,)),
            pltpu.SemaphoreType.DMA((32,)),
            pltpu.SemaphoreType.DMA((32,)),
            pltpu.SemaphoreType.REGULAR((4,)),
        ],
        compiler_params=pltpu.CompilerParams(
            collective_id=0, has_side_effects=True, vmem_limit_bytes=64 * 1024 * 1024 - 65536
        ),
    )(
        queries_in, classifier, targets.reshape(pairs, 128), owner_ids, local_ids,
    )
    return loss[0], feat, weight


def solution(mesh):
    in_specs = (
        P(("queries", "labels"), None),
        P("labels", None),
        P(("queries", "labels"), None),
        P(("queries", "labels"), None),
        P(("queries", "labels"), None, None),
    )
    out_specs = (
        P(("queries", "labels")),
        P(("queries", "labels"), None),
        P(("labels", "queries"), None),
    )
    return jax.shard_map(shards, mesh=mesh, in_specs=in_specs, out_specs=out_specs, check_vma=False)
```

```python
import jax
import jax.numpy as jnp
from jax import lax
from jax.experimental import pallas as pl
from jax.experimental.pallas import tpu as pltpu
from jax.sharding import PartitionSpec as P

MESH = pl.DeviceIdType.MESH
BF = jnp.bfloat16
F32 = jnp.float32

ORDER = [
    (0, 0), (0, 1), (1, 0), (0, 2), (2, 0), (1, 1), (1, 3), (3, 1),
    (3, 3), (2, 1), (1, 2), (2, 3), (3, 2), (2, 2), (0, 3), (3, 0),
]
SLOT = {chip: k for k, chip in enumerate(ORDER)}
MIRROR = [SLOT[(b, a)] for a, b in ORDER]
PAY = 144


def slot(a, b):
    return SLOT[(a % 4, b % 4)]


def nt(a, b):
    return lax.dot_general(a, b, (((1,), (1,)), ((), ())), preferred_element_type=F32)


def nn(a, b):
    return jnp.dot(a, b, preferred_element_type=F32)


def tn(a, b):
    return lax.dot_general(a, b, (((0,), (0,)), ((), ())), preferred_element_type=F32)


def pick_of(pay, core, k):
    spot = lax.broadcasted_iota(jnp.int32, (128, 128), 0).astype(F32) + 1.0
    tail = pay[core, k, 128:144, :].astype(F32)
    return jnp.concatenate(
        [jnp.where(spot == tail[r : r + 1, :], 1.0, 0.0) for r in (1, 2)], axis=1
    ).astype(BF)


def make_grads(k, own, sib, pay, w, grads, g_all, ids_all, loss_out):
    picks = [pick_of(pay, core, k) for core in (0, 1)]
    x = jnp.concatenate(
        [nn(picks[core], src[k]).astype(BF) for core, src in enumerate((own, sib))], axis=0
    )
    sib[k] = x
    ids = jnp.concatenate(
        [pay[core, k, 128:144, :].astype(F32)[0:1, :] for core in (0, 1)], axis=1
    )
    z = jnp.zeros((128, 256), F32)
    for part in range(2):
        scores = nt(w[part * 1024 : part * 1024 + 1024, :], x)
        for b in range(8):
            z = jnp.where(ids == float(part * 8 + b + 1), scores[b * 128 : b * 128 + 128, :], z)
    z = z.astype(BF).astype(F32)
    y = jnp.concatenate([pay[core, k, 0:128, :] for core in (0, 1)], axis=1).astype(F32)
    valid = jnp.where(ids > 0.5, 0.25, 0.0)
    e = jnp.exp(-jnp.abs(z))
    loss = jnp.sum(jnp.maximum(z, 0.0) + jnp.log1p(e) - y * z, axis=0, keepdims=True) * valid
    sig = jnp.where(z >= 0.0, 1.0, e) / (1.0 + e)
    g = ((sig - y) * valid).astype(BF)
    many = jnp.broadcast_to(ids, (16, 256))
    g_all[k] = g
    ids_all[k] = many
    g = g.reshape(8, 16, 256)
    for b in range(16):
        hot = jnp.where(many == float(b + 1), 1.0, 0.0).astype(BF)
        grads[b * 128 : b * 128 + 128, :] = (g * hot[None]).reshape(128, 256)
    place = lax.broadcasted_iota(jnp.int32, (16, 128), 0)
    for core in (0, 1):
        part = loss[:, core * 128 : core * 128 + 128]
        high = part.astype(BF).astype(F32)
        mid = (part - high).astype(BF).astype(F32)
        low = part - high - mid
        stack = jnp.where(place == 0, high, jnp.where(place == 1, mid, jnp.where(place == 2, low, 0.0)))
        spread = nn(stack.astype(BF), picks[core])
        loss_out[core, k] = jnp.broadcast_to(jnp.sum(spread, axis=0, keepdims=True), (8, 256))


def make_terms(k, pay, w, grads, terms0, terms1, index):
    f = tn(grads[...], w[...]).astype(BF)
    terms0[k] = tn(pick_of(pay, 0, k), f[0:128, :]).astype(BF)
    terms1[index] = tn(pick_of(pay, 1, k), f[128:256, :]).astype(BF)


def weight_shard(first, count, sib, g_all, ids_all, wide, total):
    def step(j, _):
        for i in range(4):
            k = j * 4 + i
            many = ids_all[k]
            g = g_all[k].reshape(8, 16, 256)
            for b in range(count):
                hot = jnp.where(many == (first + (b + 1)).astype(F32), 1.0, 0.0).astype(BF)
                wide[b * 128 : b * 128 + 128, i * 256 : i * 256 + 256] = (g * hot[None]).reshape(128, 256)
        size = count * 128
        x = sib[pl.ds(j * 4, 4)].reshape(1024, 768)
        total[0:size, :] += nn(wide[0:size, :], x)
        return 0

    total[...] = jnp.zeros_like(total)
    lax.fori_loop(0, 4, step, 0)


def kernel(
    q_ref, w, targets, owner_ref, local_ref,
    loss_ref, feat_ref, weight_ref,
    own, sib, pay_out, pay, terms0, terms1, back, half_in, full_in, half_a, full_a,
    total, half_x, full_x, shards_x, wide, g_all, ids_all, grads0, grads1,
    loss_out, loss_in, labels_in, slots,
    own_s, own_r, sib_s, sib_r, pay_s, pay_r, back_s, back_r, rs_s, rs_r, loss_s, loss_r, x_s, x_r, known,
):
    me = lax.axis_index("labels")
    mx = lax.axis_index("queries")
    core = lax.rem(me, 2)
    my = lax.rem(me // 2, 4)
    mz = me // 8

    def dev(a, b, c=0):
        dz = a * (1 - core) + b * core
        dy = b * (1 - core) + a * core
        return (lax.rem(mz + dz, 4) * 4 + lax.rem(my + dy, 4)) * 2 + lax.rem(core + c, 2)

    def to(device, src, dst, ssem, rsem):
        return pltpu.make_async_remote_copy(
            src_ref=src, dst_ref=dst, send_sem=ssem, recv_sem=rsem,
            device_id={"labels": device}, device_id_type=MESH,
        )

    def to_x(step, src, dst, ssem, rsem):
        return pltpu.make_async_remote_copy(
            src_ref=src, dst_ref=dst, send_sem=ssem, recv_sem=rsem,
            device_id={"queries": lax.rem(mx + step, 4)}, device_id_type=MESH,
        )

    barrier = pltpu.get_barrier_semaphore()
    ring_a, ring_b = (dev(1, 0), dev(3, 0)), (dev(0, 1), dev(0, 3))
    for device in (*ring_a, *ring_b, dev(0, 0, 1)):
        pl.semaphore_signal(barrier, inc=1, device_id={"labels": device}, device_id_type=MESH)
    for step in (1, 3):
        pl.semaphore_signal(
            barrier, inc=1, device_id={"queries": lax.rem(mx + step, 4)}, device_id_type=MESH
        )
    pl.semaphore_wait(barrier, 7)

    def tell(index, devices):
        for device in devices:
            pl.semaphore_signal(
                known.at[index], inc=1, device_id={"labels": device}, device_id_type=MESH
            )

    def hear(index, count):
        pl.semaphore_wait(known.at[index], count)

    sent = []

    def go(make):
        make().start()
        sent.append(make)

    def rows_of(ref, half):
        return ref if half is None else ref.at[pl.ds(half * 128, 128), :]

    def pass_on(*slots):
        sends = []
        for k in slots:
            a, b = ORDER[k]
            if b == 0:
                if a == 0:
                    sends += [(k, 1, 0, None), (k, 3, 0, None)]
                if a == 3:
                    sends.append((k, 1, 0, 0))
                if a == 1:
                    sends.append((k, 3, 0, 1))
                sends += [(k, 0, 1, None), (k, 0, 3, None)]
            if b == 3:
                sends.append((k, 0, 1, 0))
            if b == 1:
                sends.append((k, 0, 3, 1))
        sends.sort(key=lambda send: send[3] is None)
        for n, (k, sa, sb, half) in enumerate(sends):
            a, b = ORDER[k]
            there = slot(a - sa, b - sb)
            index = k * 4 + [send for send in sends if send[0] == k].index((k, sa, sb, half))
            go(
                lambda k=k, sa=sa, sb=sb, half=half, there=there, index=index: to(
                    dev(sa, sb),
                    rows_of(own.at[k], half),
                    rows_of(own.at[there], half),
                    own_s.at[index],
                    own_r.at[there * 2 + (half or 0)],
                )
            )
        for k in slots:
            go(
                lambda k=k: to(
                    dev(0, 0, 1), own.at[k], sib.at[MIRROR[k]], sib_s.at[k], sib_r.at[MIRROR[k]]
                )
            )

    def arrive(*slots):
        for k in slots:
            a, b = ORDER[k]
            halves = (0, 1) if b == 2 or (b == 0 and a == 2) else (None,)
            for half in halves:
                ref = rows_of(own.at[k], half)
                to(dev(0, 0, 1), ref, ref, own_s.at[k * 4], own_r.at[k * 2 + (half or 0)]).wait_recv()
        pass_on(*slots)

    own[0] = q_ref[...]
    pass_on(0)

    tell(0, ring_a)
    owners = owner_ref[...]
    line = lax.broadcasted_iota(jnp.int32, (32, 256), 0)
    hit = jnp.zeros((32, 256), F32)
    for t in range(8):
        hit = jnp.where(line == owners[t : t + 1, :], 1.0, hit)
    before = jnp.where(
        lax.broadcasted_iota(jnp.int32, (256, 256), 0) < lax.broadcasted_iota(jnp.int32, (256, 256), 1),
        1.0, 0.0,
    )
    rank = nn(hit.astype(BF), before.astype(BF))
    slots[...] = jnp.where(hit > 0.5, rank + 1.0, 0.0)
    columns = jnp.concatenate(
        [local_ref[...].astype(F32) + 1.0, jnp.zeros((120, 256), F32)], axis=0
    ).T
    for t in range(8):
        at = slice(t * 256, t * 256 + 256)
        labels_in[at, 0:128] = targets[pl.ds(t, 256, stride=8), :].astype(BF)
        labels_in[at, 128:256] = jnp.broadcast_to(columns[:, t : t + 1], (256, 128)).astype(BF)
    hear(0, 2)
    tell(1, ring_b)
    spot = lax.broadcasted_iota(jnp.int32, (128, 256), 0).astype(F32) + 1.0
    place = lax.broadcasted_iota(jnp.int32, (16, 128), 0)

    def pack(group, _):
        stacks = []
        for i in range(4):
            o = group * 4 + i
            mine = slots[pl.ds(o, 1), :]
            stacks.append(
                jnp.concatenate(
                    [
                        jnp.where(
                            spot == jnp.where(owners[t : t + 1, :] == o, mine, 0.0), 1.0, 0.0
                        ).astype(BF)
                        for t in range(8)
                    ],
                    axis=1,
                )
            )
        found = nn(jnp.concatenate(stacks, axis=0), labels_in[...])
        for i in range(4):
            o = group * 4 + i
            piece = found[i * 128 : i * 128 + 128, :]
            pay_out[o, 0:128, :] = piece[:, 0:128].T.astype(BF)
            ids = piece[:, 128:256].T[0:16, :]
            mine = slots[pl.ds(o, 1), :]
            tail = jnp.where(
                place == 0, ids,
                jnp.where(place == 1, mine[:, 0:128], jnp.where(place == 2, mine[:, 128:256], 0.0)),
            )
            pay_out[o, 128:144, :] = tail.astype(BF)
        return 0

    lax.fori_loop(0, 4, pack, 0)
    hear(1, 2)
    tell(2, ring_b)
    lax.fori_loop(4, 8, pack, 0)
    hear(2, 2)
    tell(3, (dev(0, 0, 1),))
    hear(3, 1)
    pay[0, 0] = pay_out[me]

    def targets_to(wanted):
        for there in wanted:
            for c in (0, 1):
                if there == 0 and c == 0:
                    continue
                a, b = ORDER[there]
                a, b = (-a % 4, -b % 4) if c == 0 else (-b % 4, -a % 4)

                def make(a=a, b=b, c=c, there=there):
                    d = dev(a, b, c)
                    return to(
                        d, pay_out.at[d], pay.at[c, there], pay_s.at[c * 16 + there], pay_r.at[c * 16 + there]
                    )

                go(make)

    def halves_of(buf, index, a_axis, store, sem):
        for h in (0, 1):
            step = 1 if h == 0 else 3
            d = (step, 0) if a_axis else (0, step)
            go(
                lambda d=d, h=h: to(
                    dev(*d), rows_of(buf.at[index], h), store(h), rs_s.at[sem + h], rs_r.at[sem + h]
                )
            )

    def full_of(h, index, a_axis, store, sem):
        step = 1 if h == 0 else 3
        d = (step, 0) if a_axis else (0, step)
        go(
            lambda: to(dev(*d), buf_at(index), store(h), rs_s.at[sem + 2 + h], rs_r.at[sem + 2 + h])
        )

    def buf_at(index):
        return terms0.at[index]

    def got(store, h, sem):
        to(dev(0, 0, 1), store(h), store(h), rs_s.at[sem], rs_r.at[sem]).wait_recv()

    def summed(a, b):
        k = slot(a, b)
        far = MIRROR[k]
        to(dev(0, 0, 1), back.at[far], back.at[far], back_s.at[far], back_r.at[far]).wait_recv()
        terms0[k] = terms0[k] + back[far]

    def far(a):
        summed(a, 2)
        halves_of(terms0, slot(a, 2), False, lambda h: half_in.at[a, h], a * 4)

    def meet(h, index, store, sem):
        got(store, h, sem + h)
        at = slice(h * 128, h * 128 + 128)
        terms0[index, at, :] = terms0[index, at, :] + store(h)[...]

    def near(a, h):
        index = slot(a, 1 if h == 0 else 3)
        summed(a, 1 if h == 0 else 3)
        meet(h, index, lambda h: half_in.at[a, h], a * 4)
        full_of(h, index, False, lambda h: full_in.at[a, h], a * 4)

    def here(a):
        summed(a, 0)
        for h in (0, 1):
            got(lambda h: full_in.at[a, h], h, a * 4 + 2 + h)
        k = slot(a, 0)
        terms0[k] = (
            terms0[k].astype(F32) + full_in[a, 0].astype(F32) + full_in[a, 1].astype(F32)
        ).astype(BF)

    def arrivals(*chips):
        arrive(*[slot(a, b) for a, b in chips])

    acts = {
        0: [lambda: targets_to(range(0, 5)), lambda: arrivals((0, 1), (1, 0), (0, 3), (3, 0))],
        1: [lambda: targets_to(range(5, 8))],
        2: [lambda: targets_to(range(8, 10)), lambda: arrivals((2, 0), (0, 2))],
        3: [lambda: targets_to(range(10, 13))],
        4: [lambda: targets_to(range(13, 16)), lambda: arrivals((1, 1), (1, 3), (3, 1), (3, 3))],
        6: [lambda: arrivals((2, 1), (2, 3))],
        8: [lambda: arrivals((1, 2), (3, 2)), lambda: far(0)],
        10: [lambda: near(0, 0)],
        11: [lambda: arrivals((2, 2))],
        12: [lambda: far(1)],
        14: [lambda: near(1, 0), lambda: near(1, 1), lambda: far(3)],
        15: [lambda: far(2)],
    }

    def send_back(k, index):
        return to(dev(0, 0, 1), terms1.at[index], back.at[k], back_s.at[k], back_r.at[k])

    all_grads = (grads0, grads1)
    grads1[...] = jnp.zeros_like(grads1)

    def step(j, _):
        for i in range(2):
            k = j * 2 + i
            for when, todo in acts.items():
                if when % 2 != i:
                    continue

                @pl.when(j == when // 2)
                def _():
                    for act in todo:
                        act()

            to(dev(0, 0, 1), sib.at[k], sib.at[k], sib_s.at[k], sib_r.at[k]).wait_recv()
            to(dev(0, 0, 1), pay.at[1, k], pay.at[1, k], pay_s.at[16 + k], pay_r.at[16 + k]).wait_recv()

            def mine():
                to(dev(0, 0, 1), pay.at[0, k], pay.at[0, k], pay_s.at[k], pay_r.at[k]).wait_recv()

            if i == 0:
                pl.when(j > 0)(mine)
            else:
                mine()

            last = lax.rem(k + 3, 4)

            @pl.when(k >= 5)
            def _():
                send_back(k - 5, last).wait_send()

            make_grads(k, own, sib, pay, w, all_grads[i], g_all, ids_all, loss_out)
            make_terms(k - 1 + lax.div(16 - k, 16), pay, w, all_grads[1 - i], terms0, terms1, last)

            def give():
                send_back(k - 1, last).start()

            if i == 0:
                pl.when(j > 0)(give)
            else:
                give()
        return 0

    lax.fori_loop(0, 8, step, 0)
    send_back(11, 3).wait_send()
    make_terms(15, pay, w, grads1, terms0, terms1, 3)
    send_back(15, 3).start()

    def shard(dx):
        weight_shard(lax.rem(mx + dx, 4) * 4, 4, sib, g_all, ids_all, wide, total)
        for h in (0, 1):
            shards_x[dx, h] = total[h * 256 : h * 256 + 256, :].astype(BF)

    def x_send(dx, h, part, store, sem):
        go(lambda: to_x(dx, shards_x.at[part, h], store(), x_s.at[sem], x_r.at[sem]))

    def x_wait(store, sem):
        to_x(1, store, store, x_s.at[sem], x_r.at[sem]).wait_recv()

    shard(2)
    x_send(1, 0, 2, lambda: half_x.at[0], 0)
    x_send(3, 1, 2, lambda: half_x.at[1], 1)
    near(2, 0)
    near(2, 1)
    near(3, 0)
    near(3, 1)
    near(0, 1)
    for k, (a, b) in enumerate(ORDER):
        for c in (0, 1):
            if k == 0 and c == 0:
                continue
            there = slot(-a, -b) if c == 0 else slot(-b, -a)
            go(
                lambda a=a, b=b, c=c, k=k, there=there: to(
                    dev(a, b, c), loss_out.at[c, k], loss_in.at[c, there],
                    loss_s.at[c * 16 + k], loss_r.at[c * 16 + there],
                )
            )
    here(2)
    halves_of(terms0, slot(2, 0), True, lambda h: half_a.at[h], 16)
    shard(1)
    x_send(1, 1, 1, lambda: full_x.at[0, 1], 3)
    here(1)
    here(3)
    meet(0, slot(1, 0), lambda h: half_a.at[h], 16)
    full_of(0, slot(1, 0), True, lambda h: full_a.at[h], 16)
    meet(1, slot(3, 0), lambda h: half_a.at[h], 16)
    full_of(1, slot(3, 0), True, lambda h: full_a.at[h], 16)
    shard(3)
    x_send(3, 0, 3, lambda: full_x.at[1, 0], 4)
    x_wait(half_x.at[0], 0)
    shards_x[1, 0] = shards_x[1, 0] + half_x[0]
    x_send(1, 0, 1, lambda: full_x.at[0, 0], 2)
    x_wait(half_x.at[1], 1)
    shards_x[3, 1] = shards_x[3, 1] + half_x[1]
    x_send(3, 1, 3, lambda: full_x.at[1, 1], 5)
    weight_shard(mx * 4, 4, sib, g_all, ids_all, wide, total)
    here(0)
    loss = loss_out[0, 0]
    for k in range(16):
        for c in (0, 1):
            if k == 0 and c == 0:
                continue
            ref = loss_in.at[c, k]
            to(dev(0, 0, 1), ref, ref, loss_s.at[c * 16 + k], loss_r.at[c * 16 + k]).wait_recv()
            loss = loss + loss_in[c, k]
    loss_ref[...] = loss[0:1, :]

    for h in (0, 1):
        got(lambda h: full_a.at[h], h, 18 + h)
    feat_ref[...] = terms0[0].astype(F32) + full_a[0].astype(F32) + full_a[1].astype(F32)

    for d in (0, 1):
        for h in (0, 1):
            x_wait(full_x.at[d, h], 2 + d * 2 + h)
    for h in (0, 1):
        weight_ref[h * 256 : h * 256 + 256, :] = (
            total[h * 256 : h * 256 + 256, :] + full_x[0, h].astype(F32) + full_x[1, h].astype(F32)
        ).astype(BF)

    for k in range(12, 16):
        send_back(k, k % 4).wait_send()
    for make in sent:
        make().wait_send()


def shards(queries_in, classifier, owner_ids, local_ids, targets):
    rows, width = queries_in.shape
    top = owner_ids.shape[1]
    pairs = rows * top
    vmem = pl.BlockSpec(memory_space=pltpu.VMEM)
    block = (rows, width)
    loss, feat, weight = pl.pallas_call(
        kernel,
        out_shape=(
            jax.ShapeDtypeStruct((1, rows), F32),
            jax.ShapeDtypeStruct(block, F32),
            jax.ShapeDtypeStruct((512, width), BF),
        ),
        in_specs=[vmem] * 5,
        out_specs=(vmem, vmem, vmem),
        scratch_shapes=[
            pltpu.VMEM((16, *block), BF),
            pltpu.VMEM((16, *block), BF),
            pltpu.VMEM((32, PAY, 128), BF),
            pltpu.VMEM((2, 16, PAY, 128), BF),
            pltpu.VMEM((16, *block), BF),
            pltpu.VMEM((4, *block), BF),
            pltpu.VMEM((16, *block), BF),
            pltpu.VMEM((4, 2, 128, width), BF),
            pltpu.VMEM((4, 2, *block), BF),
            pltpu.VMEM((2, 128, width), BF),
            pltpu.VMEM((2, *block), BF),
            pltpu.VMEM((512, width), F32),
            pltpu.VMEM((2, 256, width), BF),
            pltpu.VMEM((2, 2, 256, width), BF),
            pltpu.VMEM((4, 2, 256, width), BF),
            pltpu.VMEM((512, 1024), BF),
            pltpu.VMEM((16, 128, 256), BF),
            pltpu.VMEM((16, 16, 256), F32),
            *[pltpu.VMEM((2048, 256), BF)] * 2,
            pltpu.VMEM((2, 16, 8, rows), F32),
            pltpu.VMEM((2, 16, 8, rows), F32),
            pltpu.VMEM((pairs, 256), BF),
            pltpu.VMEM((32, rows), F32),
            pltpu.SemaphoreType.DMA((64,)),
            pltpu.SemaphoreType.DMA((32,)),
            pltpu.SemaphoreType.DMA((16,)),
            pltpu.SemaphoreType.DMA((16,)),
            pltpu.SemaphoreType.DMA((32,)),
            pltpu.SemaphoreType.DMA((32,)),
            pltpu.SemaphoreType.DMA((16,)),
            pltpu.SemaphoreType.DMA((16,)),
            pltpu.SemaphoreType.DMA((20,)),
            pltpu.SemaphoreType.DMA((20,)),
            pltpu.SemaphoreType.DMA((32,)),
            pltpu.SemaphoreType.DMA((32,)),
            pltpu.SemaphoreType.DMA((6,)),
            pltpu.SemaphoreType.DMA((6,)),
            pltpu.SemaphoreType.REGULAR((4,)),
        ],
        compiler_params=pltpu.CompilerParams(
            collective_id=0, has_side_effects=True, vmem_limit_bytes=64 * 1024 * 1024 - 65536
        ),
    )(
        queries_in, classifier, targets.reshape(pairs, 128), owner_ids.T, local_ids.T,
    )
    return loss.reshape(rows), feat, weight


def solution(mesh):
    in_specs = (
        P(("queries", "labels"), None),
        P("labels", None),
        P(("queries", "labels"), None),
        P(("queries", "labels"), None),
        P(("queries", "labels"), None, None),
    )
    out_specs = (
        P(("queries", "labels")),
        P(("queries", "labels"), None),
        P(("labels", "queries"), None),
    )
    return jax.shard_map(shards, mesh=mesh, in_specs=in_specs, out_specs=out_specs, check_vma=False)
```

```python
import jax
import jax.numpy as jnp
from jax import lax
from jax.experimental import pallas as pl
from jax.experimental.pallas import tpu as pltpu
from jax.sharding import PartitionSpec as P

MESH = pl.DeviceIdType.MESH
BF = jnp.bfloat16
F32 = jnp.float32

ORDER = [
    (0, 0), (0, 1), (1, 0), (0, 2), (2, 0), (1, 1), (1, 3), (3, 1),
    (3, 3), (2, 1), (1, 2), (2, 3), (3, 2), (2, 2), (0, 3), (3, 0),
]
SLOT = {chip: k for k, chip in enumerate(ORDER)}
MIRROR = [SLOT[(b, a)] for a, b in ORDER]
PAY = 144


def slot(a, b):
    return SLOT[(a % 4, b % 4)]


def nt(a, b):
    return lax.dot_general(a, b, (((1,), (1,)), ((), ())), preferred_element_type=F32)


def nn(a, b):
    return jnp.dot(a, b, preferred_element_type=F32)


def tn(a, b):
    return lax.dot_general(a, b, (((0,), (0,)), ((), ())), preferred_element_type=F32)


def pick_of(pay, core, k):
    spot = lax.broadcasted_iota(jnp.int32, (128, 128), 0).astype(F32) + 1.0
    tail = pay[core, k, 128:144, :].astype(F32)
    return jnp.concatenate(
        [jnp.where(spot == tail[r : r + 1, :], 1.0, 0.0) for r in (1, 2)], axis=1
    ).astype(BF)


def make_grads(k, own, sib, pay, w, grads, g_all, ids_all, loss_out, k1, grads1, terms0, terms1, index):
    picks = [pick_of(pay, core, k) for core in (0, 1)]
    x = jnp.concatenate(
        [nn(picks[core], src[k]).astype(BF) for core, src in enumerate((own, sib))], axis=0
    )
    sib[k] = x
    ids = jnp.concatenate(
        [pay[core, k, 128:144, :].astype(F32)[0:1, :] for core in (0, 1)], axis=1
    )
    z = jnp.zeros((128, 256), F32)
    f = jnp.zeros((256, 768), F32)
    for part in range(2):
        at = slice(part * 1024, part * 1024 + 1024)
        scores = nt(w[at, :], x)
        f = f + tn(grads1[at, :], w[at, :])
        for b in range(8):
            z = jnp.where(ids == float(part * 8 + b + 1), scores[b * 128 : b * 128 + 128, :], z)
    z = z.astype(BF).astype(F32)
    y = jnp.concatenate([pay[core, k, 0:128, :] for core in (0, 1)], axis=1).astype(F32)
    valid = jnp.where(ids > 0.5, 0.25, 0.0)
    f = f.astype(BF)
    terms0[k1] = tn(pick_of(pay, 0, k1), f[0:128, :]).astype(BF)
    terms1[index] = tn(pick_of(pay, 1, k1), f[128:256, :]).astype(BF)
    e = jnp.exp(-jnp.abs(z))
    loss = jnp.sum(jnp.maximum(z, 0.0) + jnp.log1p(e) - y * z, axis=0, keepdims=True) * valid
    sig = jnp.where(z >= 0.0, 1.0, e) / (1.0 + e)
    g = ((sig - y) * valid).astype(BF)
    many = jnp.broadcast_to(ids, (16, 256))
    g_all[k] = g
    ids_all[k] = many
    g = g.reshape(8, 16, 256)
    for b in range(16):
        hot = jnp.where(many == float(b + 1), 1.0, 0.0).astype(BF)
        grads[b * 128 : b * 128 + 128, :] = (g * hot[None]).reshape(128, 256)
    place = lax.broadcasted_iota(jnp.int32, (16, 128), 0)
    for core in (0, 1):
        part = loss[:, core * 128 : core * 128 + 128]
        high = part.astype(BF).astype(F32)
        mid = (part - high).astype(BF).astype(F32)
        low = part - high - mid
        stack = jnp.where(place == 0, high, jnp.where(place == 1, mid, jnp.where(place == 2, low, 0.0)))
        spread = nn(stack.astype(BF), picks[core])
        loss_out[core, k] = jnp.broadcast_to(jnp.sum(spread, axis=0, keepdims=True), (8, 256))


def make_terms(k, pay, w, grads, terms0, terms1, index):
    f = tn(grads[...], w[...]).astype(BF)
    terms0[k] = tn(pick_of(pay, 0, k), f[0:128, :]).astype(BF)
    terms1[index] = tn(pick_of(pay, 1, k), f[128:256, :]).astype(BF)


def weight_step(first, j, sib, g_all, ids_all, wide, total):
    for i in range(4):
        k = j * 4 + i
        many = ids_all[k]
        g = g_all[k].reshape(8, 16, 256)
        for b in range(4):
            hot = jnp.where(many == (first + (b + 1)).astype(F32), 1.0, 0.0).astype(BF)
            wide[b * 128 : b * 128 + 128, i * 256 : i * 256 + 256] = (g * hot[None]).reshape(128, 256)
    x = sib[pl.ds(j * 4, 4)].reshape(1024, 768)
    total[...] += nn(wide[...], x)


def kernel(
    q_ref, w, targets, owner_ref, local_ref,
    loss_ref, feat_ref, weight_ref,
    own, sib, pay_out, pay, terms0, terms1, back, half_in, full_in, half_a, full_a,
    total, half_x, full_x, shards_x, wide, g_all, ids_all, grads0, grads1,
    loss_out, loss_in, labels_in, slots,
    own_s, own_r, sib_s, sib_r, pay_s, pay_r, back_s, back_r, rs_s, rs_r, loss_s, loss_r, x_s, x_r, known,
):
    me = lax.axis_index("labels")
    mx = lax.axis_index("queries")
    core = lax.rem(me, 2)
    my = lax.rem(me // 2, 4)
    mz = me // 8

    def dev(a, b, c=0):
        dz = a * (1 - core) + b * core
        dy = b * (1 - core) + a * core
        return (lax.rem(mz + dz, 4) * 4 + lax.rem(my + dy, 4)) * 2 + lax.rem(core + c, 2)

    def to(device, src, dst, ssem, rsem):
        return pltpu.make_async_remote_copy(
            src_ref=src, dst_ref=dst, send_sem=ssem, recv_sem=rsem,
            device_id={"labels": device}, device_id_type=MESH,
        )

    def to_x(step, src, dst, ssem, rsem):
        return pltpu.make_async_remote_copy(
            src_ref=src, dst_ref=dst, send_sem=ssem, recv_sem=rsem,
            device_id={"queries": lax.rem(mx + step, 4)}, device_id_type=MESH,
        )

    barrier = pltpu.get_barrier_semaphore()
    ring_a, ring_b = (dev(1, 0), dev(3, 0)), (dev(0, 1), dev(0, 3))
    for device in (*ring_a, *ring_b, dev(0, 0, 1)):
        pl.semaphore_signal(barrier, inc=1, device_id={"labels": device}, device_id_type=MESH)
    for step in (1, 3):
        pl.semaphore_signal(
            barrier, inc=1, device_id={"queries": lax.rem(mx + step, 4)}, device_id_type=MESH
        )
    pl.semaphore_wait(barrier, 7)

    def tell(index, devices):
        for device in devices:
            pl.semaphore_signal(
                known.at[index], inc=1, device_id={"labels": device}, device_id_type=MESH
            )

    def hear(index, count):
        pl.semaphore_wait(known.at[index], count)

    sent = []

    def go(make):
        make().start()
        sent.append(make)

    def rows_of(ref, half):
        return ref if half is None else ref.at[pl.ds(half * 128, 128), :]

    def pass_on(*slots):
        sends = []
        for k in slots:
            a, b = ORDER[k]
            if b == 0:
                if a == 0:
                    sends += [(k, 1, 0, None), (k, 3, 0, None)]
                if a == 3:
                    sends.append((k, 1, 0, 0))
                if a == 1:
                    sends.append((k, 3, 0, 1))
                sends += [(k, 0, 1, None), (k, 0, 3, None)]
            if b == 3:
                sends.append((k, 0, 1, 0))
            if b == 1:
                sends.append((k, 0, 3, 1))
        sends.sort(key=lambda send: send[3] is None)
        for n, (k, sa, sb, half) in enumerate(sends):
            a, b = ORDER[k]
            there = slot(a - sa, b - sb)
            index = k * 4 + [send for send in sends if send[0] == k].index((k, sa, sb, half))
            go(
                lambda k=k, sa=sa, sb=sb, half=half, there=there, index=index: to(
                    dev(sa, sb),
                    rows_of(own.at[k], half),
                    rows_of(own.at[there], half),
                    own_s.at[index],
                    own_r.at[there * 2 + (half or 0)],
                )
            )
        for k in slots:
            go(
                lambda k=k: to(
                    dev(0, 0, 1), own.at[k], sib.at[MIRROR[k]], sib_s.at[k], sib_r.at[MIRROR[k]]
                )
            )

    def arrive(*slots):
        for k in slots:
            a, b = ORDER[k]
            halves = (0, 1) if b == 2 or (b == 0 and a == 2) else (None,)
            for half in halves:
                ref = rows_of(own.at[k], half)
                to(dev(0, 0, 1), ref, ref, own_s.at[k * 4], own_r.at[k * 2 + (half or 0)]).wait_recv()
        pass_on(*slots)

    own[0] = q_ref[...]
    pass_on(0)
    total[...] = jnp.zeros_like(total)

    tell(0, ring_a)
    owners = owner_ref[...]
    line = lax.broadcasted_iota(jnp.int32, (32, 256), 0)
    hit = jnp.zeros((32, 256), F32)
    for t in range(8):
        hit = jnp.where(line == owners[t : t + 1, :], 1.0, hit)
    before = jnp.where(
        lax.broadcasted_iota(jnp.int32, (256, 256), 0) < lax.broadcasted_iota(jnp.int32, (256, 256), 1),
        1.0, 0.0,
    )
    rank = nn(hit.astype(BF), before.astype(BF))
    slots[...] = jnp.where(hit > 0.5, rank + 1.0, 0.0)
    columns = jnp.concatenate(
        [local_ref[...].astype(F32) + 1.0, jnp.zeros((120, 256), F32)], axis=0
    ).T
    for t in range(8):
        at = slice(t * 256, t * 256 + 256)
        labels_in[at, 0:128] = targets[pl.ds(t, 256, stride=8), :].astype(BF)
        labels_in[at, 128:256] = jnp.broadcast_to(columns[:, t : t + 1], (256, 128)).astype(BF)
    hear(0, 2)
    tell(1, ring_b)
    spot = lax.broadcasted_iota(jnp.int32, (128, 256), 0).astype(F32) + 1.0
    place = lax.broadcasted_iota(jnp.int32, (16, 128), 0)

    def pack(group, _):
        stacks = []
        for i in range(4):
            o = group * 4 + i
            mine = slots[pl.ds(o, 1), :]
            stacks.append(
                jnp.concatenate(
                    [
                        jnp.where(
                            spot == jnp.where(owners[t : t + 1, :] == o, mine, 0.0), 1.0, 0.0
                        ).astype(BF)
                        for t in range(8)
                    ],
                    axis=1,
                )
            )
        found = nn(jnp.concatenate(stacks, axis=0), labels_in[...])
        for i in range(4):
            o = group * 4 + i
            piece = found[i * 128 : i * 128 + 128, :]
            pay_out[o, 0:128, :] = piece[:, 0:128].T.astype(BF)
            ids = piece[:, 128:256].T[0:16, :]
            mine = slots[pl.ds(o, 1), :]
            tail = jnp.where(
                place == 0, ids,
                jnp.where(place == 1, mine[:, 0:128], jnp.where(place == 2, mine[:, 128:256], 0.0)),
            )
            pay_out[o, 128:144, :] = tail.astype(BF)
        return 0

    lax.fori_loop(0, 3, pack, 0)
    hear(1, 2)
    tell(2, ring_b)
    lax.fori_loop(3, 6, pack, 0)
    hear(2, 2)
    tell(3, (dev(0, 0, 1),))
    lax.fori_loop(6, 8, pack, 0)
    hear(3, 1)
    pay[0, 0] = pay_out[me]

    def targets_to(wanted):
        for there in wanted:
            for c in (0, 1):
                if there == 0 and c == 0:
                    continue
                a, b = ORDER[there]
                a, b = (-a % 4, -b % 4) if c == 0 else (-b % 4, -a % 4)

                def make(a=a, b=b, c=c, there=there):
                    d = dev(a, b, c)
                    return to(
                        d, pay_out.at[d], pay.at[c, there], pay_s.at[c * 16 + there], pay_r.at[c * 16 + there]
                    )

                go(make)

    def halves_of(buf, index, a_axis, store, sem):
        for h in (0, 1):
            step = 1 if h == 0 else 3
            d = (step, 0) if a_axis else (0, step)
            go(
                lambda d=d, h=h: to(
                    dev(*d), rows_of(buf.at[index], h), store(h), rs_s.at[sem + h], rs_r.at[sem + h]
                )
            )

    def full_of(h, index, a_axis, store, sem):
        step = 1 if h == 0 else 3
        d = (step, 0) if a_axis else (0, step)
        go(
            lambda: to(dev(*d), buf_at(index), store(h), rs_s.at[sem + 2 + h], rs_r.at[sem + 2 + h])
        )

    def buf_at(index):
        return terms0.at[index]

    def got(store, h, sem):
        to(dev(0, 0, 1), store(h), store(h), rs_s.at[sem], rs_r.at[sem]).wait_recv()

    def summed(a, b):
        k = slot(a, b)
        far = MIRROR[k]
        to(dev(0, 0, 1), back.at[far], back.at[far], back_s.at[far], back_r.at[far]).wait_recv()
        terms0[k] = terms0[k] + back[far]

    def far(a):
        summed(a, 2)
        halves_of(terms0, slot(a, 2), False, lambda h: half_in.at[a, h], a * 4)

    def meet(h, index, store, sem):
        got(store, h, sem + h)
        at = slice(h * 128, h * 128 + 128)
        terms0[index, at, :] = terms0[index, at, :] + store(h)[...]

    def near(a, h):
        index = slot(a, 1 if h == 0 else 3)
        summed(a, 1 if h == 0 else 3)
        meet(h, index, lambda h: half_in.at[a, h], a * 4)
        full_of(h, index, False, lambda h: full_in.at[a, h], a * 4)

    def here(a):
        summed(a, 0)
        for h in (0, 1):
            got(lambda h: full_in.at[a, h], h, a * 4 + 2 + h)
        k = slot(a, 0)
        terms0[k] = (
            terms0[k].astype(F32) + full_in[a, 0].astype(F32) + full_in[a, 1].astype(F32)
        ).astype(BF)

    def arrivals(*chips):
        arrive(*[slot(a, b) for a, b in chips])

    acts = {
        0: [lambda: targets_to(range(0, 5)), lambda: arrivals((0, 1), (1, 0), (0, 3), (3, 0))],
        1: [lambda: targets_to(range(5, 8))],
        2: [lambda: targets_to(range(8, 10)), lambda: arrivals((2, 0), (0, 2))],
        3: [lambda: targets_to(range(10, 13))],
        4: [lambda: targets_to(range(13, 16)), lambda: arrivals((1, 1), (1, 3), (3, 1), (3, 3))],
        6: [lambda: arrivals((2, 1), (2, 3))],
        8: [lambda: arrivals((1, 2), (3, 2)), lambda: far(0)],
        10: [lambda: near(0, 0)],
        11: [lambda: arrivals((2, 2))],
        12: [lambda: far(1)],
        14: [lambda: near(1, 0), lambda: near(1, 1), lambda: far(3)],
        15: [lambda: far(2)],
    }

    def send_back(k, index):
        return to(dev(0, 0, 1), terms1.at[index], back.at[k], back_s.at[k], back_r.at[k])

    all_grads = (grads0, grads1)
    grads1[...] = jnp.zeros_like(grads1)

    def weights(dx, j):
        weight_step(lax.rem(mx + dx, 4) * 4, j, sib, g_all, ids_all, wide, total.at[dx])

    def step(j, _):
        for i in range(2):
            k = j * 2 + i
            for when, todo in acts.items():
                if when % 2 != i:
                    continue

                @pl.when(j == when // 2)
                def _():
                    for act in todo:
                        act()

            to(dev(0, 0, 1), sib.at[k], sib.at[k], sib_s.at[k], sib_r.at[k]).wait_recv()
            to(dev(0, 0, 1), pay.at[1, k], pay.at[1, k], pay_s.at[16 + k], pay_r.at[16 + k]).wait_recv()

            def mine():
                to(dev(0, 0, 1), pay.at[0, k], pay.at[0, k], pay_s.at[k], pay_r.at[k]).wait_recv()

            if i == 0:
                pl.when(j > 0)(mine)
            else:
                mine()

            last = lax.rem(k + 3, 4)

            @pl.when(k >= 5)
            def _():
                send_back(k - 5, last).wait_send()

            make_grads(
                k, own, sib, pay, w, all_grads[i], g_all, ids_all, loss_out,
                k - 1 + lax.div(16 - k, 16), all_grads[1 - i], terms0, terms1, last,
            )

            def give():
                send_back(k - 1, last).start()

            if i == 0:
                pl.when(j > 0)(give)
            else:
                give()

            @pl.when(k >= 4)
            def _():
                weights(lax.rem(k, 4), k // 4 - 1)

        return 0

    lax.fori_loop(0, 8, step, 0)
    send_back(11, 3).wait_send()
    make_terms(15, pay, w, grads1, terms0, terms1, 3)
    send_back(15, 3).start()

    def shard(dx):
        weights(dx, 3)
        for h in (0, 1):
            shards_x[dx, h] = total[dx, h * 256 : h * 256 + 256, :].astype(BF)

    def x_send(dx, h, part, store, sem):
        go(lambda: to_x(dx, shards_x.at[part, h], store(), x_s.at[sem], x_r.at[sem]))

    def x_wait(store, sem):
        to_x(1, store, store, x_s.at[sem], x_r.at[sem]).wait_recv()

    shard(2)
    x_send(1, 0, 2, lambda: half_x.at[0], 0)
    x_send(3, 1, 2, lambda: half_x.at[1], 1)
    near(2, 0)
    near(2, 1)
    near(3, 0)
    near(3, 1)
    near(0, 1)
    shard(1)
    x_send(1, 1, 1, lambda: full_x.at[0, 1], 3)
    shard(3)
    x_send(3, 0, 3, lambda: full_x.at[1, 0], 4)
    for k, (a, b) in enumerate(ORDER):
        for c in (0, 1):
            if k == 0 and c == 0:
                continue
            there = slot(-a, -b) if c == 0 else slot(-b, -a)
            go(
                lambda a=a, b=b, c=c, k=k, there=there: to(
                    dev(a, b, c), loss_out.at[c, k], loss_in.at[c, there],
                    loss_s.at[c * 16 + k], loss_r.at[c * 16 + there],
                )
            )
    here(2)
    halves_of(terms0, slot(2, 0), True, lambda h: half_a.at[h], 16)
    here(1)
    x_wait(half_x.at[0], 0)
    shards_x[1, 0] = shards_x[1, 0] + half_x[0]
    x_send(1, 0, 1, lambda: full_x.at[0, 0], 2)
    x_wait(half_x.at[1], 1)
    shards_x[3, 1] = shards_x[3, 1] + half_x[1]
    x_send(3, 1, 3, lambda: full_x.at[1, 1], 5)
    meet(0, slot(1, 0), lambda h: half_a.at[h], 16)
    full_of(0, slot(1, 0), True, lambda h: full_a.at[h], 16)
    here(3)
    meet(1, slot(3, 0), lambda h: half_a.at[h], 16)
    full_of(1, slot(3, 0), True, lambda h: full_a.at[h], 16)
    weights(0, 3)
    here(0)
    loss = loss_out[0, 0]
    for k in range(16):
        for c in (0, 1):
            if k == 0 and c == 0:
                continue
            ref = loss_in.at[c, k]
            to(dev(0, 0, 1), ref, ref, loss_s.at[c * 16 + k], loss_r.at[c * 16 + k]).wait_recv()
            loss = loss + loss_in[c, k]
    loss_ref[...] = loss[0:1, :]

    for h in (0, 1):
        got(lambda h: full_a.at[h], h, 18 + h)
    feat_ref[...] = terms0[0].astype(F32) + full_a[0].astype(F32) + full_a[1].astype(F32)

    for d in (0, 1):
        for h in (0, 1):
            x_wait(full_x.at[d, h], 2 + d * 2 + h)
    for h in (0, 1):
        weight_ref[h * 256 : h * 256 + 256, :] = (
            total[0, h * 256 : h * 256 + 256, :] + full_x[0, h].astype(F32) + full_x[1, h].astype(F32)
        ).astype(BF)

    for k in range(12, 16):
        send_back(k, k % 4).wait_send()
    for make in sent:
        make().wait_send()


def shards(queries_in, classifier, owner_ids, local_ids, targets):
    rows, width = queries_in.shape
    top = owner_ids.shape[1]
    pairs = rows * top
    vmem = pl.BlockSpec(memory_space=pltpu.VMEM)
    block = (rows, width)
    loss, feat, weight = pl.pallas_call(
        kernel,
        out_shape=(
            jax.ShapeDtypeStruct((1, rows), F32),
            jax.ShapeDtypeStruct(block, F32),
            jax.ShapeDtypeStruct((512, width), BF),
        ),
        in_specs=[vmem] * 5,
        out_specs=(vmem, vmem, vmem),
        scratch_shapes=[
            pltpu.VMEM((16, *block), BF),
            pltpu.VMEM((16, *block), BF),
            pltpu.VMEM((32, PAY, 128), BF),
            pltpu.VMEM((2, 16, PAY, 128), BF),
            pltpu.VMEM((16, *block), BF),
            pltpu.VMEM((4, *block), BF),
            pltpu.VMEM((16, *block), BF),
            pltpu.VMEM((4, 2, 128, width), BF),
            pltpu.VMEM((4, 2, *block), BF),
            pltpu.VMEM((2, 128, width), BF),
            pltpu.VMEM((2, *block), BF),
            pltpu.VMEM((4, 512, width), F32),
            pltpu.VMEM((2, 256, width), BF),
            pltpu.VMEM((2, 2, 256, width), BF),
            pltpu.VMEM((4, 2, 256, width), BF),
            pltpu.VMEM((512, 1024), BF),
            pltpu.VMEM((16, 128, 256), BF),
            pltpu.VMEM((16, 16, 256), F32),
            *[pltpu.VMEM((2048, 256), BF)] * 2,
            pltpu.VMEM((2, 16, 8, rows), F32),
            pltpu.VMEM((2, 16, 8, rows), F32),
            pltpu.VMEM((pairs, 256), BF),
            pltpu.VMEM((32, rows), F32),
            pltpu.SemaphoreType.DMA((64,)),
            pltpu.SemaphoreType.DMA((32,)),
            pltpu.SemaphoreType.DMA((16,)),
            pltpu.SemaphoreType.DMA((16,)),
            pltpu.SemaphoreType.DMA((32,)),
            pltpu.SemaphoreType.DMA((32,)),
            pltpu.SemaphoreType.DMA((16,)),
            pltpu.SemaphoreType.DMA((16,)),
            pltpu.SemaphoreType.DMA((20,)),
            pltpu.SemaphoreType.DMA((20,)),
            pltpu.SemaphoreType.DMA((32,)),
            pltpu.SemaphoreType.DMA((32,)),
            pltpu.SemaphoreType.DMA((6,)),
            pltpu.SemaphoreType.DMA((6,)),
            pltpu.SemaphoreType.REGULAR((4,)),
        ],
        compiler_params=pltpu.CompilerParams(
            collective_id=0, has_side_effects=True, vmem_limit_bytes=64 * 1024 * 1024 - 65536
        ),
    )(
        queries_in, classifier, targets.reshape(pairs, 128), owner_ids.T, local_ids.T,
    )
    return loss.reshape(rows), feat, weight


def solution(mesh):
    in_specs = (
        P(("queries", "labels"), None),
        P("labels", None),
        P(("queries", "labels"), None),
        P(("queries", "labels"), None),
        P(("queries", "labels"), None, None),
    )
    out_specs = (
        P(("queries", "labels")),
        P(("queries", "labels"), None),
        P(("labels", "queries"), None),
    )
    return jax.shard_map(shards, mesh=mesh, in_specs=in_specs, out_specs=out_specs, check_vma=False)
```

```python
import jax
import jax.numpy as jnp
from jax import lax
from jax.experimental import pallas as pl
from jax.experimental.pallas import tpu as pltpu
from jax.sharding import PartitionSpec as P

MESH = pl.DeviceIdType.MESH
BF = jnp.bfloat16
F32 = jnp.float32

ORDER = [
    (0, 0), (0, 1), (1, 0), (0, 2), (2, 0), (1, 1), (1, 3), (3, 1),
    (3, 3), (2, 1), (1, 2), (2, 2), (2, 3), (3, 2), (0, 3), (3, 0),
]
SLOT = {chip: k for k, chip in enumerate(ORDER)}
MIRROR = [SLOT[(b, a)] for a, b in ORDER]
PAY = 144


def slot(a, b):
    return SLOT[(a % 4, b % 4)]


def nt(a, b):
    return lax.dot_general(a, b, (((1,), (1,)), ((), ())), preferred_element_type=F32)


def nn(a, b):
    return jnp.dot(a, b, preferred_element_type=F32)


def tn(a, b):
    return lax.dot_general(a, b, (((0,), (0,)), ((), ())), preferred_element_type=F32)


def pick_of(pay, core, k):
    spot = lax.broadcasted_iota(jnp.int32, (128, 128), 0).astype(F32) + 1.0
    tail = pay[core, k, 128:144, :].astype(F32)
    return jnp.concatenate(
        [jnp.where(spot == tail[r : r + 1, :], 1.0, 0.0) for r in (1, 2)], axis=1
    ).astype(BF)


def make_grads(k, own, sib, pay, w, grads, g_all, ids_all, loss_out, k1, grads1, terms0, terms1, index):
    picks = [pick_of(pay, core, k) for core in (0, 1)]
    x = jnp.concatenate(
        [nn(picks[core], src[k]).astype(BF) for core, src in enumerate((own, sib))], axis=0
    )
    sib[k] = x
    ids = jnp.concatenate(
        [pay[core, k, 128:144, :].astype(F32)[0:1, :] for core in (0, 1)], axis=1
    )
    z = jnp.zeros((128, 256), F32)
    f = jnp.zeros((256, 768), F32)
    for part in range(2):
        at = slice(part * 1024, part * 1024 + 1024)
        scores = nt(w[at, :], x)
        f = f + tn(grads1[at, :], w[at, :])
        for b in range(8):
            z = jnp.where(ids == float(part * 8 + b + 1), scores[b * 128 : b * 128 + 128, :], z)
    z = z.astype(BF).astype(F32)
    y = jnp.concatenate([pay[core, k, 0:128, :] for core in (0, 1)], axis=1).astype(F32)
    valid = jnp.where(ids > 0.5, 0.25, 0.0)
    f = f.astype(BF)
    terms0[k1] = tn(pick_of(pay, 0, k1), f[0:128, :]).astype(BF)
    terms1[index] = tn(pick_of(pay, 1, k1), f[128:256, :]).astype(BF)
    e = jnp.exp(-jnp.abs(z))
    loss = jnp.sum(jnp.maximum(z, 0.0) + jnp.log1p(e) - y * z, axis=0, keepdims=True) * valid
    sig = jnp.where(z >= 0.0, 1.0, e) / (1.0 + e)
    g = ((sig - y) * valid).astype(BF)
    many = jnp.broadcast_to(ids, (16, 256))
    g_all[k] = g
    ids_all[k] = many
    g = g.reshape(8, 16, 256)
    for b in range(16):
        hot = jnp.where(many == float(b + 1), 1.0, 0.0).astype(BF)
        grads[b * 128 : b * 128 + 128, :] = (g * hot[None]).reshape(128, 256)
    place = lax.broadcasted_iota(jnp.int32, (16, 128), 0)
    for core in (0, 1):
        part = loss[:, core * 128 : core * 128 + 128]
        high = part.astype(BF).astype(F32)
        mid = (part - high).astype(BF).astype(F32)
        low = part - high - mid
        stack = jnp.where(place == 0, high, jnp.where(place == 1, mid, jnp.where(place == 2, low, 0.0)))
        spread = nn(stack.astype(BF), picks[core])
        loss_out[core, k] = jnp.broadcast_to(jnp.sum(spread, axis=0, keepdims=True), (8, 256))


def make_terms(k, pay, w, grads, terms0, terms1, index):
    f = tn(grads[...], w[...]).astype(BF)
    terms0[k] = tn(pick_of(pay, 0, k), f[0:128, :]).astype(BF)
    terms1[index] = tn(pick_of(pay, 1, k), f[128:256, :]).astype(BF)


def weight_step(first, j, sib, g_all, ids_all, wide, total):
    for i in range(4):
        k = j * 4 + i
        many = ids_all[k]
        g = g_all[k].reshape(8, 16, 256)
        for b in range(4):
            hot = jnp.where(many == (first + (b + 1)).astype(F32), 1.0, 0.0).astype(BF)
            wide[b * 128 : b * 128 + 128, i * 256 : i * 256 + 256] = (g * hot[None]).reshape(128, 256)
    x = sib[pl.ds(j * 4, 4)].reshape(1024, 768)
    total[...] += nn(wide[...], x)


def kernel(
    q_ref, w, targets, owner_ref, local_ref,
    loss_ref, feat_ref, weight_ref,
    own, sib, pay_out, pay, terms0, terms1, back, half_in, full_in, half_a, full_a,
    total, half_x, full_x, shards_x, wide, g_all, ids_all, grads0, grads1,
    loss_out, loss_in, labels_in, slots,
    own_s, own_r, sib_s, sib_r, pay_s, pay_r, back_s, back_r, rs_s, rs_r, loss_s, loss_r, x_s, x_r, known,
):
    me = lax.axis_index("labels")
    mx = lax.axis_index("queries")
    core = lax.rem(me, 2)
    my = lax.rem(me // 2, 4)
    mz = me // 8

    def dev(a, b, c=0):
        dz = a * (1 - core) + b * core
        dy = b * (1 - core) + a * core
        return (lax.rem(mz + dz, 4) * 4 + lax.rem(my + dy, 4)) * 2 + lax.rem(core + c, 2)

    def to(device, src, dst, ssem, rsem):
        return pltpu.make_async_remote_copy(
            src_ref=src, dst_ref=dst, send_sem=ssem, recv_sem=rsem,
            device_id={"labels": device}, device_id_type=MESH,
        )

    def to_x(step, src, dst, ssem, rsem):
        return pltpu.make_async_remote_copy(
            src_ref=src, dst_ref=dst, send_sem=ssem, recv_sem=rsem,
            device_id={"queries": lax.rem(mx + step, 4)}, device_id_type=MESH,
        )

    barrier = pltpu.get_barrier_semaphore()
    ring_a, ring_b = (dev(1, 0), dev(3, 0)), (dev(0, 1), dev(0, 3))
    for device in (*ring_a, *ring_b, dev(0, 0, 1)):
        pl.semaphore_signal(barrier, inc=1, device_id={"labels": device}, device_id_type=MESH)
    for step in (1, 3):
        pl.semaphore_signal(
            barrier, inc=1, device_id={"queries": lax.rem(mx + step, 4)}, device_id_type=MESH
        )
    pl.semaphore_wait(barrier, 7)

    def tell(index, devices):
        for device in devices:
            pl.semaphore_signal(
                known.at[index], inc=1, device_id={"labels": device}, device_id_type=MESH
            )

    def hear(index, count):
        pl.semaphore_wait(known.at[index], count)

    sent = []

    def go(make):
        make().start()
        sent.append(make)

    def rows_of(ref, half):
        return ref if half is None else ref.at[pl.ds(half * 128, 128), :]

    def pass_on(*slots):
        sends = []
        for k in slots:
            a, b = ORDER[k]
            if b == 0:
                if a == 0:
                    sends += [(k, 1, 0, None), (k, 3, 0, None)]
                if a == 3:
                    sends.append((k, 1, 0, 0))
                if a == 1:
                    sends.append((k, 3, 0, 1))
                sends += [(k, 0, 1, None), (k, 0, 3, None)]
            if b == 3:
                sends.append((k, 0, 1, 0))
            if b == 1:
                sends.append((k, 0, 3, 1))
        sends.sort(key=lambda send: send[3] is None)
        for n, (k, sa, sb, half) in enumerate(sends):
            a, b = ORDER[k]
            there = slot(a - sa, b - sb)
            index = k * 4 + [send for send in sends if send[0] == k].index((k, sa, sb, half))
            go(
                lambda k=k, sa=sa, sb=sb, half=half, there=there, index=index: to(
                    dev(sa, sb),
                    rows_of(own.at[k], half),
                    rows_of(own.at[there], half),
                    own_s.at[index],
                    own_r.at[there * 2 + (half or 0)],
                )
            )
        for k in slots:
            go(
                lambda k=k: to(
                    dev(0, 0, 1), own.at[k], sib.at[MIRROR[k]], sib_s.at[k], sib_r.at[MIRROR[k]]
                )
            )

    def arrive(*slots):
        for k in slots:
            a, b = ORDER[k]
            halves = (0, 1) if b == 2 or (b == 0 and a == 2) else (None,)
            for half in halves:
                ref = rows_of(own.at[k], half)
                to(dev(0, 0, 1), ref, ref, own_s.at[k * 4], own_r.at[k * 2 + (half or 0)]).wait_recv()
        pass_on(*slots)

    own[0] = q_ref[...]
    pass_on(0)
    total[...] = jnp.zeros_like(total)

    tell(0, ring_a)
    owners = owner_ref[...]
    line = lax.broadcasted_iota(jnp.int32, (32, 256), 0)
    hit = jnp.zeros((32, 256), F32)
    for t in range(8):
        hit = jnp.where(line == owners[t : t + 1, :], 1.0, hit)
    before = jnp.where(
        lax.broadcasted_iota(jnp.int32, (256, 256), 0) < lax.broadcasted_iota(jnp.int32, (256, 256), 1),
        1.0, 0.0,
    )
    rank = nn(hit.astype(BF), before.astype(BF))
    slots[...] = jnp.where(hit > 0.5, rank + 1.0, 0.0)
    columns = jnp.concatenate(
        [local_ref[...].astype(F32) + 1.0, jnp.zeros((120, 256), F32)], axis=0
    ).T
    for t in range(8):
        at = slice(t * 256, t * 256 + 256)
        labels_in[at, 0:128] = targets[pl.ds(t, 256, stride=8), :].astype(BF)
        labels_in[at, 128:256] = jnp.broadcast_to(columns[:, t : t + 1], (256, 128)).astype(BF)
    hear(0, 2)
    tell(1, ring_b)
    spot = lax.broadcasted_iota(jnp.int32, (128, 256), 0).astype(F32) + 1.0
    place = lax.broadcasted_iota(jnp.int32, (16, 128), 0)

    def pack(group, _):
        stacks = []
        for i in range(4):
            o = group * 4 + i
            mine = slots[pl.ds(o, 1), :]
            stacks.append(
                jnp.concatenate(
                    [
                        jnp.where(
                            spot == jnp.where(owners[t : t + 1, :] == o, mine, 0.0), 1.0, 0.0
                        ).astype(BF)
                        for t in range(8)
                    ],
                    axis=1,
                )
            )
        found = nn(jnp.concatenate(stacks, axis=0), labels_in[...])
        for i in range(4):
            o = group * 4 + i
            piece = found[i * 128 : i * 128 + 128, :]
            pay_out[o, 0:128, :] = piece[:, 0:128].T.astype(BF)
            ids = piece[:, 128:256].T[0:16, :]
            mine = slots[pl.ds(o, 1), :]
            tail = jnp.where(
                place == 0, ids,
                jnp.where(place == 1, mine[:, 0:128], jnp.where(place == 2, mine[:, 128:256], 0.0)),
            )
            pay_out[o, 128:144, :] = tail.astype(BF)
        return 0

    lax.fori_loop(0, 3, pack, 0)
    hear(1, 2)
    tell(2, ring_b)
    lax.fori_loop(3, 6, pack, 0)
    hear(2, 2)
    tell(3, (dev(0, 0, 1),))
    lax.fori_loop(6, 8, pack, 0)
    hear(3, 1)
    pay[0, 0] = pay_out[me]

    def targets_to(wanted):
        for there in wanted:
            for c in (0, 1):
                if there == 0 and c == 0:
                    continue
                a, b = ORDER[there]
                a, b = (-a % 4, -b % 4) if c == 0 else (-b % 4, -a % 4)

                def make(a=a, b=b, c=c, there=there):
                    d = dev(a, b, c)
                    return to(
                        d, pay_out.at[d], pay.at[c, there], pay_s.at[c * 16 + there], pay_r.at[c * 16 + there]
                    )

                go(make)

    def halves_of(buf, index, a_axis, store, sem):
        for h in (0, 1):
            step = 1 if h == 0 else 3
            d = (step, 0) if a_axis else (0, step)
            go(
                lambda d=d, h=h: to(
                    dev(*d), rows_of(buf.at[index], h), store(h), rs_s.at[sem + h], rs_r.at[sem + h]
                )
            )

    def full_of(h, index, a_axis, store, sem):
        step = 1 if h == 0 else 3
        d = (step, 0) if a_axis else (0, step)
        go(
            lambda: to(dev(*d), buf_at(index), store(h), rs_s.at[sem + 2 + h], rs_r.at[sem + 2 + h])
        )

    def buf_at(index):
        return terms0.at[index]

    def got(store, h, sem):
        to(dev(0, 0, 1), store(h), store(h), rs_s.at[sem], rs_r.at[sem]).wait_recv()

    def summed(a, b):
        k = slot(a, b)
        far = MIRROR[k]
        to(dev(0, 0, 1), back.at[far], back.at[far], back_s.at[far], back_r.at[far]).wait_recv()
        terms0[k] = terms0[k] + back[far]

    def far(a):
        summed(a, 2)
        halves_of(terms0, slot(a, 2), False, lambda h: half_in.at[a, h], a * 4)

    def meet(h, index, store, sem):
        got(store, h, sem + h)
        at = slice(h * 128, h * 128 + 128)
        terms0[index, at, :] = terms0[index, at, :] + store(h)[...]

    def near(a, h):
        index = slot(a, 1 if h == 0 else 3)
        summed(a, 1 if h == 0 else 3)
        meet(h, index, lambda h: half_in.at[a, h], a * 4)
        full_of(h, index, False, lambda h: full_in.at[a, h], a * 4)

    def here(a):
        summed(a, 0)
        for h in (0, 1):
            got(lambda h: full_in.at[a, h], h, a * 4 + 2 + h)
        k = slot(a, 0)
        terms0[k] = (
            terms0[k].astype(F32) + full_in[a, 0].astype(F32) + full_in[a, 1].astype(F32)
        ).astype(BF)

    def arrivals(*chips):
        arrive(*[slot(a, b) for a, b in chips])

    acts = {
        0: [lambda: targets_to(range(0, 5)), lambda: arrivals((0, 1), (1, 0), (0, 3), (3, 0))],
        1: [lambda: targets_to(range(5, 8))],
        2: [lambda: targets_to(range(8, 10)), lambda: arrivals((2, 0), (0, 2))],
        3: [lambda: targets_to(range(10, 13))],
        4: [lambda: targets_to(range(13, 16)), lambda: arrivals((1, 1), (1, 3), (3, 1), (3, 3))],
        6: [lambda: arrivals((2, 1), (2, 3))],
        8: [lambda: arrivals((1, 2), (3, 2)), lambda: far(0)],
        10: [lambda: near(0, 0), lambda: arrivals((2, 2))],
        12: [lambda: far(1)],
        13: [lambda: far(2)],
        14: [lambda: near(1, 0), lambda: near(1, 1)],
        15: [lambda: near(2, 0), lambda: far(3)],
    }

    def send_back(k, index):
        return to(dev(0, 0, 1), terms1.at[index], back.at[k], back_s.at[k], back_r.at[k])

    all_grads = (grads0, grads1)
    grads1[...] = jnp.zeros_like(grads1)

    def weights(dx, j):
        weight_step(lax.rem(mx + dx, 4) * 4, j, sib, g_all, ids_all, wide, total.at[dx])

    def step(j, _):
        for i in range(2):
            k = j * 2 + i
            for when, todo in acts.items():
                if when % 2 != i:
                    continue

                @pl.when(j == when // 2)
                def _():
                    for act in todo:
                        act()

            to(dev(0, 0, 1), sib.at[k], sib.at[k], sib_s.at[k], sib_r.at[k]).wait_recv()
            to(dev(0, 0, 1), pay.at[1, k], pay.at[1, k], pay_s.at[16 + k], pay_r.at[16 + k]).wait_recv()

            def mine():
                to(dev(0, 0, 1), pay.at[0, k], pay.at[0, k], pay_s.at[k], pay_r.at[k]).wait_recv()

            if i == 0:
                pl.when(j > 0)(mine)
            else:
                mine()

            last = lax.rem(k + 3, 4)

            @pl.when(k >= 5)
            def _():
                send_back(k - 5, last).wait_send()

            make_grads(
                k, own, sib, pay, w, all_grads[i], g_all, ids_all, loss_out,
                k - 1 + lax.div(16 - k, 16), all_grads[1 - i], terms0, terms1, last,
            )

            def give():
                send_back(k - 1, last).start()

            if i == 0:
                pl.when(j > 0)(give)
            else:
                give()

            @pl.when(k >= 4)
            def _():
                weights(lax.rem(k, 4), k // 4 - 1)

        return 0

    lax.fori_loop(0, 8, step, 0)

    def shard(dx):
        weights(dx, 3)
        for h in (0, 1):
            shards_x[dx, h] = total[dx, h * 256 : h * 256 + 256, :].astype(BF)

    def x_send(dx, h, part, store, sem):
        go(lambda: to_x(dx, shards_x.at[part, h], store(), x_s.at[sem], x_r.at[sem]))

    def x_wait(store, sem):
        to_x(1, store, store, x_s.at[sem], x_r.at[sem]).wait_recv()

    shard(2)
    x_send(1, 0, 2, lambda: half_x.at[0], 0)
    x_send(3, 1, 2, lambda: half_x.at[1], 1)
    send_back(11, 3).wait_send()
    make_terms(15, pay, w, grads1, terms0, terms1, 3)
    send_back(15, 3).start()
    near(2, 1)
    near(3, 0)
    near(3, 1)
    near(0, 1)
    shard(1)
    x_send(1, 1, 1, lambda: full_x.at[0, 1], 3)
    shard(3)
    x_send(3, 0, 3, lambda: full_x.at[1, 0], 4)
    for k, (a, b) in enumerate(ORDER):
        for c in (0, 1):
            if k == 0 and c == 0:
                continue
            there = slot(-a, -b) if c == 0 else slot(-b, -a)
            go(
                lambda a=a, b=b, c=c, k=k, there=there: to(
                    dev(a, b, c), loss_out.at[c, k], loss_in.at[c, there],
                    loss_s.at[c * 16 + k], loss_r.at[c * 16 + there],
                )
            )
    here(2)
    halves_of(terms0, slot(2, 0), True, lambda h: half_a.at[h], 16)
    here(1)
    x_wait(half_x.at[0], 0)
    shards_x[1, 0] = shards_x[1, 0] + half_x[0]
    x_send(1, 0, 1, lambda: full_x.at[0, 0], 2)
    x_wait(half_x.at[1], 1)
    shards_x[3, 1] = shards_x[3, 1] + half_x[1]
    x_send(3, 1, 3, lambda: full_x.at[1, 1], 5)
    meet(0, slot(1, 0), lambda h: half_a.at[h], 16)
    full_of(0, slot(1, 0), True, lambda h: full_a.at[h], 16)
    here(3)
    meet(1, slot(3, 0), lambda h: half_a.at[h], 16)
    full_of(1, slot(3, 0), True, lambda h: full_a.at[h], 16)
    weights(0, 3)
    here(0)
    loss = loss_out[0, 0]
    for k in range(16):
        for c in (0, 1):
            if k == 0 and c == 0:
                continue
            ref = loss_in.at[c, k]
            to(dev(0, 0, 1), ref, ref, loss_s.at[c * 16 + k], loss_r.at[c * 16 + k]).wait_recv()
            loss = loss + loss_in[c, k]
    loss_ref[...] = loss[0:1, :]

    for h in (0, 1):
        got(lambda h: full_a.at[h], h, 18 + h)
    feat_ref[...] = terms0[0].astype(F32) + full_a[0].astype(F32) + full_a[1].astype(F32)

    for d in (0, 1):
        for h in (0, 1):
            x_wait(full_x.at[d, h], 2 + d * 2 + h)
    for h in (0, 1):
        weight_ref[h * 256 : h * 256 + 256, :] = (
            total[0, h * 256 : h * 256 + 256, :] + full_x[0, h].astype(F32) + full_x[1, h].astype(F32)
        ).astype(BF)

    for k in range(12, 16):
        send_back(k, k % 4).wait_send()
    for make in sent:
        make().wait_send()


def shards(queries_in, classifier, owner_ids, local_ids, targets):
    rows, width = queries_in.shape
    top = owner_ids.shape[1]
    pairs = rows * top
    vmem = pl.BlockSpec(memory_space=pltpu.VMEM)
    block = (rows, width)
    loss, feat, weight = pl.pallas_call(
        kernel,
        out_shape=(
            jax.ShapeDtypeStruct((1, rows), F32),
            jax.ShapeDtypeStruct(block, F32),
            jax.ShapeDtypeStruct((512, width), BF),
        ),
        in_specs=[vmem] * 5,
        out_specs=(vmem, vmem, vmem),
        scratch_shapes=[
            pltpu.VMEM((16, *block), BF),
            pltpu.VMEM((16, *block), BF),
            pltpu.VMEM((32, PAY, 128), BF),
            pltpu.VMEM((2, 16, PAY, 128), BF),
            pltpu.VMEM((16, *block), BF),
            pltpu.VMEM((4, *block), BF),
            pltpu.VMEM((16, *block), BF),
            pltpu.VMEM((4, 2, 128, width), BF),
            pltpu.VMEM((4, 2, *block), BF),
            pltpu.VMEM((2, 128, width), BF),
            pltpu.VMEM((2, *block), BF),
            pltpu.VMEM((4, 512, width), F32),
            pltpu.VMEM((2, 256, width), BF),
            pltpu.VMEM((2, 2, 256, width), BF),
            pltpu.VMEM((4, 2, 256, width), BF),
            pltpu.VMEM((512, 1024), BF),
            pltpu.VMEM((16, 128, 256), BF),
            pltpu.VMEM((16, 16, 256), F32),
            *[pltpu.VMEM((2048, 256), BF)] * 2,
            pltpu.VMEM((2, 16, 8, rows), F32),
            pltpu.VMEM((2, 16, 8, rows), F32),
            pltpu.VMEM((pairs, 256), BF),
            pltpu.VMEM((32, rows), F32),
            pltpu.SemaphoreType.DMA((64,)),
            pltpu.SemaphoreType.DMA((32,)),
            pltpu.SemaphoreType.DMA((16,)),
            pltpu.SemaphoreType.DMA((16,)),
            pltpu.SemaphoreType.DMA((32,)),
            pltpu.SemaphoreType.DMA((32,)),
            pltpu.SemaphoreType.DMA((16,)),
            pltpu.SemaphoreType.DMA((16,)),
            pltpu.SemaphoreType.DMA((20,)),
            pltpu.SemaphoreType.DMA((20,)),
            pltpu.SemaphoreType.DMA((32,)),
            pltpu.SemaphoreType.DMA((32,)),
            pltpu.SemaphoreType.DMA((6,)),
            pltpu.SemaphoreType.DMA((6,)),
            pltpu.SemaphoreType.REGULAR((4,)),
        ],
        compiler_params=pltpu.CompilerParams(
            collective_id=0, has_side_effects=True, vmem_limit_bytes=64 * 1024 * 1024 - 65536
        ),
    )(
        queries_in, classifier, targets.reshape(pairs, 128), owner_ids.T, local_ids.T,
    )
    return loss.reshape(rows), feat, weight


def solution(mesh):
    in_specs = (
        P(("queries", "labels"), None),
        P("labels", None),
        P(("queries", "labels"), None),
        P(("queries", "labels"), None),
        P(("queries", "labels"), None, None),
    )
    out_specs = (
        P(("queries", "labels")),
        P(("queries", "labels"), None),
        P(("labels", "queries"), None),
    )
    return jax.shard_map(shards, mesh=mesh, in_specs=in_specs, out_specs=out_specs, check_vma=False)
```
